128 devices in a mesh: rep: 64 (over x, z, y_lo, core), shard: 2 (over y_hi).
Axes of the slice: x: 4, y: 4 (y_hi: 2, y_lo: 2; y = y_hi * 2 + y_lo), z: 4, core: 2. Of those that a mesh axis runs over, the one named last changes fastest.
Arguments:
- tokens: bfloat16 [32768, 768], P(('rep', 'shard')), may hold values from -6 to 6
- w_qkv: bfloat16 [768, 2304], P('shard'), may hold values from -0.21875 to 0.21875
- b_qv: bfloat16 [1536], P('shard'), may hold values from -3 to 3
- w_out: bfloat16 [768, 768], P('shard'), may hold values from -0.875 to 0.875
- b_out: bfloat16 [768], P('shard'), may hold values from -3 to 3
- w_up: bfloat16 [768, 3072], P('shard'), may hold values from -0.21875 to 0.21875
- b_up: bfloat16 [3072], P('shard'), may hold values from -3 to 3
- w_down: bfloat16 [3072, 768], P('shard'), may hold values from -0.109375 to 0.109375
- b_down: bfloat16 [768], P('shard'), may hold values from -3 to 3
- gain_one: bfloat16 [768], P('shard'), may hold values from 0.5 to 1.5
- shift_one: bfloat16 [768], P('shard'), may hold values from -2 to 2
- gain_two: bfloat16 [768], P('shard'), may hold values from 0.5 to 1.5
- shift_two: bfloat16 [768], P('shard'), may hold values from -2 to 2
- cotangent: bfloat16 [32768, 768], P(('rep', 'shard')), may hold values from -6 to 6
Outputs:
- result: bfloat16 [32768, 768], P(('rep', 'shard'))
- input_grad: float32 [32768, 768], P(('rep', 'shard'))
- grad_w_qkv: float32 [768, 2304], P('shard')
- grad_b_qv: float32 [1536], P('shard')
- grad_w_out: float32 [768, 768], P('shard')
- grad_b_out: float32 [768], P('shard')
- grad_w_up: float32 [768, 3072], P('shard')
- grad_b_up: float32 [3072], P('shard')
- grad_w_down: float32 [3072, 768], P('shard')
- grad_b_down: float32 [768], P('shard')
- grad_gain_one: float32 [768], P('shard')
- grad_shift_one: float32 [768], P('shard')
- grad_gain_two: float32 [768], P('shard')
- grad_shift_two: float32 [768], P('shard')
The draws below stay inside these ranges and needn't reach their ends.
All inputs are finite; a program needn't handle non-finite values.
Results may differ from the reference program's by a relative error of at most 0.014.
Values may be sent and summed in bfloat16 or wider, within the bound.
No kernel may reach another device: no remote copies, remote signals or barrier semaphores. Data moves between devices by JAX's collectives and lax.ppermute only.
A program may use at most 128 MiB of HBM per device.

```python
import math
import jax
import jax.numpy as jnp
from jax import lax

D = 768
HEADS = 12
HEAD_DIM = 64
FF = 3072
LENGTH = 512
TOKENS = 32768


def shard_levels(key, dims, split, least, top_value):
    def one(dim, shards_of):
        steps = jax.random.uniform(jax.random.fold_in(jax.random.fold_in(key, 6), dim), (shards_of,), jnp.float32, least / len(split), top_value / len(split))
        return jnp.repeat(jnp.exp(steps), dims[dim] // shards_of).reshape((-1,) + (1,) * (len(dims) - dim - 1))

    loudness = one(*split[0])
    for cut in split[1:]:
        loudness = loudness * one(*cut)
    return loudness


def gaussian(key, dims, width, reach, split=(), dtype=jnp.bfloat16):
    values = width * jax.random.normal(key, dims, jnp.float32)
    if split:
        values = values * shard_levels(key, dims, split, -0.22, 0.18)
    return jnp.clip(values, -reach, reach).astype(dtype)


def setup_inputs(seed: int = 0) -> dict:
    seeds = jax.random.split(jax.random.key(seed), 15)
    return {
        "tokens": gaussian(seeds[0], (TOKENS, D), 1.0, 6.0, ((0, 128),)),
        "w_qkv": gaussian(seeds[1], (D, 3 * D), D ** -0.5, 0.21875, ((0, 2),)),
        "b_qv": gaussian(seeds[2], (2 * D,), 0.5, 3.0, ((0, 2),)),
        "w_out": gaussian(seeds[3], (D, D), (D // 16) ** -0.5, 0.875, ((0, 2),)),
        "b_out": gaussian(seeds[4], (D,), 0.5, 3.0, ((0, 2),)),
        "w_up": gaussian(seeds[5], (D, FF), D ** -0.5, 0.21875, ((0, 2),)),
        "b_up": gaussian(seeds[6], (FF,), 0.5, 3.0, ((0, 2),)),
        "w_down": gaussian(seeds[7], (FF, D), FF ** -0.5, 0.109375, ((0, 2),)),
        "b_down": gaussian(seeds[8], (D,), 0.5, 3.0, ((0, 2),)),
        "gain_one": jnp.clip(1.0 + 0.1 * jax.random.normal(seeds[9], (D,), jnp.float32), 0.5, 1.5).astype(jnp.bfloat16),
        "shift_one": gaussian(seeds[10], (D,), 0.3, 2.0, ((0, 2),)),
        "gain_two": jnp.clip(1.0 + 0.1 * jax.random.normal(seeds[11], (D,), jnp.float32), 0.5, 1.5).astype(jnp.bfloat16),
        "shift_two": gaussian(seeds[12], (D,), 0.3, 2.0, ((0, 2),)),
        "cotangent": gaussian(seeds[13], (TOKENS, D), 1.0, 6.0, ((0, 128),)),
    }


@jax.custom_vjp
def low(v):
    return lax.optimization_barrier(v.astype(jnp.bfloat16)).astype(jnp.float32)

@jax.custom_vjp
def low_back(v):
    return v

def low_keep(v):
    return (low(v), None)

def low_pass(kept, grad):
    return (grad,)

def back_keep(v):
    return (v, None)

def back_low(kept, grad):
    return (low(grad),)
low.defvjp(low_keep, low_pass)
low_back.defvjp(back_keep, back_low)
eps = 1e-05

def matmul(left, right):
    return jnp.einsum('gld,de->gle', left, right, precision=lax.Precision.HIGHEST)

def layer_norm(values, gain, shift):
    center = lax.optimization_barrier(jnp.mean(values, axis=-1, keepdims=True))
    centered = values - center
    spread = lax.optimization_barrier(jnp.mean(centered * centered, axis=-1, keepdims=True))
    return centered * lax.rsqrt(spread + eps) * gain + shift

def block(params, inputs):
    w_qkv, b_qv, w_out, b_out, w_up, b_up, w_down, b_down, gain_one, shift_one, gain_two, shift_two = params
    groups = inputs.shape[0]
    length = inputs.shape[1]
    normed = low(layer_norm(inputs, gain_one, shift_one))
    projected = matmul(normed, w_qkv)
    queries = low(low_back((projected[..., :D] + b_qv[:D]) * 0.125))
    keys = low(low_back(projected[..., D:2 * D]))
    values_in = low(low_back(projected[..., 2 * D:] + b_qv[D:]))
    shape = (groups, length, HEADS, HEAD_DIM)
    scores = low_back(jnp.einsum('gqhd,gkhd->ghqk', queries.reshape(shape), keys.reshape(shape), precision=lax.Precision.HIGHEST))
    causal = jnp.arange(length)[:, None] >= jnp.arange(length)[None, :]
    scores = jnp.where(causal, scores, -1e+30)
    weights = low(jax.nn.softmax(scores, axis=-1))
    attended = jnp.einsum('ghqk,gkhd->gqhd', weights, values_in.reshape(shape), precision=lax.Precision.HIGHEST).reshape(groups, length, D)
    attended = low(low_back(attended))
    branch = low_back(matmul(attended, w_out) + b_out)
    middle = inputs + branch
    normed_two = low(layer_norm(middle, gain_two, shift_two))
    hidden = low_back(matmul(normed_two, w_up) + b_up)
    activated = low(jax.nn.gelu(hidden))
    out_branch = low_back(matmul(activated, w_down) + b_down)
    return middle + out_branch

def reference(tokens, w_qkv, b_qv, w_out, b_out, w_up, b_up, w_down, b_down, gain_one, shift_one, gain_two, shift_two, cotangent):
    group = math.gcd(TOKENS // LENGTH, max(1, 4096 // LENGTH))
    params = tuple((item.astype(jnp.float32) for item in (w_qkv, b_qv, w_out, b_out, w_up, b_up, w_down, b_down, gain_one, shift_one, gain_two, shift_two)))

    def forward(inputs, weights):
        blocks = inputs.reshape(TOKENS // (group * LENGTH), group, LENGTH, D)
        outputs = lax.map(jax.checkpoint(lambda piece: block(weights, piece)), blocks)
        return outputs.reshape(TOKENS, D)
    result, pullback = jax.vjp(forward, tokens.astype(jnp.float32), params)
    input_grad, grads = pullback(cotangent.astype(jnp.float32))
    return (result.astype(jnp.bfloat16), input_grad, grads[0], grads[1], grads[2], grads[3], grads[4], grads[5], grads[6], grads[7], grads[8], grads[9], grads[10], grads[11])
```

```python
import functools
import jax
import jax.numpy as jnp
from jax import lax
from jax.experimental import pallas as pl
from jax.experimental.pallas import tpu as pltpu
from jax.sharding import Mesh
from jax.sharding import PartitionSpec as P

HEAD_DIM = 64
eps = 1e-05
F32 = jnp.float32
BF16 = jnp.bfloat16
VMEM_LIMIT = 56 * 1024 * 1024


def dot_nn(left, right):
    return lax.dot_general(left, right, (((1,), (0,)), ((), ())), preferred_element_type=F32)


def dot_nt(left, right):
    return lax.dot_general(left, right, (((1,), (1,)), ((), ())), preferred_element_type=F32)


def dot_tn(left, right):
    return lax.dot_general(left, right, (((0,), (0,)), ((), ())), preferred_element_type=F32)


def normalise(values):
    center = jnp.mean(values, axis=-1, keepdims=True)
    centered = values - center
    spread = jnp.mean(centered * centered, axis=-1, keepdims=True)
    scale = lax.rsqrt(spread + eps)
    return centered * scale, scale


def norm_back(unit, scale, upstream, gain):
    q = upstream * gain
    return scale * (
        q
        - jnp.mean(q, axis=-1, keepdims=True)
        - unit * jnp.mean(q * unit, axis=-1, keepdims=True)
    )


def column_sum(values):
    return jnp.sum(values, axis=0, keepdims=True)


def two_heads(block):
    lane = lax.broadcasted_iota(jnp.int32, block.shape, 1)
    zero = jnp.zeros_like(block)
    return jnp.concatenate(
        [jnp.where(lane < HEAD_DIM, block, zero), jnp.where(lane < HEAD_DIM, zero, block)], axis=0
    )


def merge_heads(rows_t, count):
    row = lax.broadcasted_iota(jnp.int32, (2 * HEAD_DIM, count), 0)
    return jnp.transpose(
        jnp.where(row < HEAD_DIM, rows_t[:, :count], rows_t[:, count:]), (1, 0)
    )


def masked_scores(keys_two, queries_two, hidden_prev, count):
    scores = dot_nt(keys_two, queries_two)
    key = lax.broadcasted_iota(jnp.int32, (count, 2 * count), 0)
    query = lax.broadcasted_iota(jnp.int32, (count, 2 * count), 1)
    query = jnp.where(query >= count, query - count, query)
    prev = scores[:count] + hidden_prev
    here = jnp.where(key <= query, scores[count:], -1e30)
    return jnp.concatenate([prev, here], axis=0)


def assemble(place, parts, target, sems, first):
    own, near, far = parts
    half, quarter = own.shape[0], near.shape[0]
    shard, core = place[0], place[1]
    starts = (
        shard * half,
        (1 - shard) * half + core * quarter,
        (1 - shard) * half + (1 - core) * quarter,
    )
    copies = []
    for index, (part, start) in enumerate(zip(parts, starts)):
        rows = pl.ds(pl.multiple_of(start, quarter), part.shape[0])
        copies.append(pltpu.make_async_copy(part, target.at[rows], sems.at[first + index]))
        copies[-1].start()
    return copies


def finish(copies):
    for copy in copies:
        copy.wait()


def store_columns(target, core, chunk, value):
    blocks, wide = target.shape[3], target.shape[5]
    value = value.astype(BF16)
    for half in range(value.shape[1] // wide):
        place = chunk * (value.shape[1] // wide) + half
        block = value[:, half * wide : (half + 1) * wide].reshape(
            target.shape[1], target.shape[2], target.shape[4], wide
        )
        target[lax.rem(core + place // blocks, 2), :, :, place % blocks] = block


def forward_attention(
    place, x_prev, x_here, own, near, far, b_qv, gain, shift,
    normed, queries, keys, values, attended, log_total, w_qkv, sems,
):
    copies = assemble(place, (own, near, far), w_qkv, sems, 0)
    rows, width = x_here.shape
    hidden_prev = jnp.where(place[0] > 0, 0.0, -1e30).astype(F32)
    for part, source in enumerate((x_prev, x_here)):
        unit, _ = normalise(source[...].astype(F32))
        normed[part * rows : (part + 1) * rows, :] = (unit * gain[...] + shift[...]).astype(BF16)
    finish(copies)
    here = normed[rows:, :]
    queries[...] = ((dot_nn(here, w_qkv[:, :width]) + b_qv[:, :width]) * 0.125).astype(BF16)
    keys[...] = dot_nn(normed[...], w_qkv[:, width : 2 * width]).astype(BF16)
    values[...] = (dot_nn(normed[...], w_qkv[:, 2 * width :]) + b_qv[:, width:]).astype(BF16)
    for pair in range(width // (2 * HEAD_DIM)):
        at = slice(pair * 2 * HEAD_DIM, (pair + 1) * 2 * HEAD_DIM)
        scores = masked_scores(keys[:, at], two_heads(queries[:, at]), hidden_prev, rows)
        top = jnp.max(scores, axis=0, keepdims=True)
        expo = jnp.exp(scores - top)
        total = jnp.sum(expo, axis=0, keepdims=True)
        probs_low = (expo * (1.0 / total)).astype(BF16)
        log_total[pair : pair + 1, :] = top + jnp.log(total)
        attended[:, at] = merge_heads(dot_tn(values[:, at], probs_low), rows).astype(BF16)


def forward_middle(
    place, attended, x_here, out_own, out_near, out_far, b_out, gain, shift,
    up_own, up_near, up_far, b_up, cotangent,
    middle, normed, hidden, activated, grad_w_down, grad_b_down, w_out, w_up, sems,
):
    out_copies = assemble(place, (out_own, out_near, out_far), w_out, sems, 0)
    up_copies = assemble(place, (up_own, up_near, up_far), w_up, sems, 3)
    finish(out_copies)
    rows, width = x_here.shape
    mid = x_here[...].astype(F32) + (dot_nn(attended[...], w_out[...]) + b_out[...])
    middle[...] = mid
    unit, _ = normalise(mid)
    normed[...] = (unit * gain[...] + shift[...]).astype(BF16)
    finish(up_copies)
    for chunk in range(w_up.shape[1] // width):
        at = slice(chunk * width, (chunk + 1) * width)
        hid = dot_nn(normed[...], w_up[:, at]) + b_up[:, at]
        hidden[:, at] = hid
        low = jax.nn.gelu(hid, approximate=True).astype(BF16)
        activated[:, at] = low
        part = dot_tn(low, cotangent[...]).astype(BF16)
        grad_w_down[lax.rem(place[1] + chunk, 2), chunk // 2] = part
    grad_b_down[...] = column_sum(cotangent[...].astype(F32))


def gelu_slope(u):
    c = 0.7978845608028654
    t = jnp.tanh(c * (u + 0.044715 * (u * u * u)))
    return 0.5 * (1.0 + t) + 0.5 * u * (1.0 - t * t) * (c * (1.0 + 3.0 * 0.044715 * (u * u)))


def middle_back(
    place, cotangent, hidden, activated, normed, middle, own, near, far, b_down,
    result, grad_hidden, grad_w_up, grad_b_up, w_down, sems,
):
    finish(assemble(place, (own, near, far), w_down, sems, 0))
    rows, width = middle.shape
    ct = cotangent[...]
    out = jnp.zeros((rows, width), F32)
    for chunk in range(w_down.shape[0] // width):
        at = slice(chunk * width, (chunk + 1) * width)
        grad_act = dot_nt(ct, w_down[at, :])
        grad_hid = (grad_act * gelu_slope(hidden[:, at])).astype(BF16)
        grad_hidden[:, at] = grad_hid
        grad_b_up[:, at] = column_sum(grad_hid.astype(F32))
        store_columns(grad_w_up, place[1], chunk, dot_tn(normed[...], grad_hid))
        out = out + dot_nn(activated[:, at], w_down[at, :])
    result[...] = (middle[...] + (out + b_down[...])).astype(result.dtype)


def input_back(
    place, x_prev, x_here, cotangent, middle, grad_hidden, gain_two, attended,
    normed, queries, keys, values, log_total, gain_one,
    up_own, up_near, up_far, out_own, out_near, out_far, qkv_own, qkv_near, qkv_far,
    input_grad, prev_grad, grad_w_attn, small,
    grad_att, grad_proj, w_up, w_out, w_qkv, sems,
):
    up_copies = assemble(place, (up_own, up_near, up_far), w_up, sems, 0)
    out_copies = assemble(place, (out_own, out_near, out_far), w_out, sems, 3)
    qkv_copies = assemble(place, (qkv_own, qkv_near, qkv_far), w_qkv, sems, 6)
    finish(up_copies)
    finish(out_copies)
    finish(qkv_copies)
    rows, width = x_here.shape
    hidden_prev = jnp.where(place[0] > 0, 0.0, -1e30).astype(F32)
    grad_norm = dot_nt(grad_hidden[...], w_up[...])
    unit, scale = normalise(middle[...])
    small[4:5, :] = column_sum(grad_norm * unit)
    small[5:6, :] = column_sum(grad_norm)
    grad_mid = cotangent[...].astype(F32) + norm_back(unit, scale, grad_norm, gain_two[...])
    grad_branch = grad_mid.astype(BF16)
    input_grad[...] = grad_mid
    small[6:7, :] = column_sum(grad_branch.astype(F32))
    grad_att[...] = dot_nt(grad_branch, w_out[...]).astype(BF16)
    store_columns(grad_w_attn, place[1], 3, dot_tn(attended[...], grad_branch))
    grad_proj[:rows, :width] = jnp.zeros((rows, width), BF16)
    for pair in range(width // (2 * HEAD_DIM)):
        at = slice(pair * 2 * HEAD_DIM, (pair + 1) * 2 * HEAD_DIM)
        queries_two = two_heads(queries[:, at])
        grads_two = two_heads(grad_att[:, at])
        scores = masked_scores(keys[:, at], queries_two, hidden_prev, rows)
        probs = jnp.exp(scores - log_total[pair : pair + 1, :])
        probs_low = probs.astype(BF16)
        grad_probs = dot_nt(values[:, at], grads_two)
        inner = jnp.sum(probs * grad_probs, axis=0, keepdims=True)
        grad_scores = (probs * (grad_probs - inner)).astype(BF16)
        first, last = pair * 2 * HEAD_DIM, (pair + 1) * 2 * HEAD_DIM
        grad_queries = merge_heads(dot_tn(keys[:, at], grad_scores), rows)
        grad_proj[rows:, at] = (grad_queries.astype(BF16) * 0.125).astype(BF16)
        grad_proj[:, width + first : width + last] = dot_nn(grad_scores, queries_two).astype(BF16)
        grad_proj[:, 2 * width + first : 2 * width + last] = dot_nn(probs_low, grads_two).astype(BF16)
    for chunk in range(3):
        at = slice(chunk * width, (chunk + 1) * width)
        store_columns(grad_w_attn, place[1], chunk, dot_tn(normed[...], grad_proj[:, at]))
    small[0:1, :] = column_sum(grad_proj[:, :width].astype(F32))
    small[1:2, :] = column_sum(grad_proj[:, 2 * width :].astype(F32))
    gain_sum = jnp.zeros((1, width), F32)
    shift_sum = jnp.zeros((1, width), F32)
    for part, source in enumerate((x_prev, x_here)):
        at = slice(part * rows, (part + 1) * rows)
        first = (1 - part) * width
        grad_norm = dot_nt(grad_proj[at, first:], w_qkv[:, first:])
        unit, scale = normalise(source[...].astype(F32))
        gain_sum = gain_sum + column_sum(grad_norm * unit)
        shift_sum = shift_sum + column_sum(grad_norm)
        grad_in = norm_back(unit, scale, grad_norm, gain_one[...])
        if part == 0:
            prev_grad[...] = grad_in.astype(prev_grad.dtype)
        else:
            input_grad[...] = input_grad[...] + grad_in
    small[2:3, :] = gain_sum
    small[3:4, :] = shift_sum
    small[7:8, :] = jnp.zeros((1, width), F32)


VM = pl.BlockSpec(memory_space=pltpu.VMEM)
SM = pl.BlockSpec(memory_space=pltpu.SMEM)


def call(body, outs, flops, moved, in_specs, scratch=()):
    return pl.pallas_call(
        body,
        out_shape=tuple(jax.ShapeDtypeStruct(s, d) for s, d in outs),
        in_specs=in_specs,
        out_specs=tuple(VM for _ in outs),
        scratch_shapes=list(scratch),
        compiler_params=pltpu.CompilerParams(vmem_limit_bytes=VMEM_LIMIT),
        cost_estimate=pl.CostEstimate(flops=flops, bytes_accessed=moved, transcendentals=0),
    )


CHIPS = ("y_hi", "x", "z", "y_lo")
COPIES = ("x", "z", "y_lo")
SWAP = [(0, 1), (1, 0)]
ACROSS = [(0, 3), (1, 2), (2, 1), (3, 0)]


def fetch(shard, core):
    quarter = shard.shape[0] // 2
    mine = lax.dynamic_slice_in_dim(shard, core * quarter, quarter, 0)
    near = lax.ppermute(mine, ("y_lo", "y_hi"), ACROSS)
    far = lax.ppermute(near, "core", SWAP)
    return shard, near, far


def reduce_chunks(chunks):
    other = lax.ppermute(chunks[1], "core", SWAP)
    both = (chunks[0].astype(F32) + other.astype(F32)).astype(BF16)
    spread = lax.all_to_all(both, CHIPS, 0, 0, tiled=True)
    return jnp.sum(spread, axis=0, dtype=F32).astype(BF16)


def gather_chunks(chunk):
    copies = 1
    for axis in COPIES:
        copies *= lax.axis_size(axis)
    mine = lax.all_to_all(
        jnp.broadcast_to(chunk[None], (copies,) + chunk.shape), COPIES, 0, 0, tiled=True
    )
    return mine, lax.ppermute(mine, "core", SWAP)


def ordered(core, mine, other):
    first = jnp.where(core == 0, mine, other)
    last = jnp.where(core == 0, other, mine)
    return jnp.stack([first, last]).astype(F32)


def on_device(
    tokens, w_qkv, b_qv, w_out, b_out, w_up, b_up, w_down, b_down,
    gain_one, shift_one, gain_two, shift_two, cotangent,
):
    rows, width = tokens.shape
    ff = w_up.shape[1]
    shard = lax.axis_index("y_hi")
    core = lax.axis_index("core")
    place = jnp.stack([shard, core]).astype(jnp.int32)
    x_prev = lax.ppermute(tokens, "y_hi", [(0, 1)])
    vectors = (b_qv, b_out, b_down, gain_one, shift_one, gain_two, shift_two, b_up)
    packed = jnp.concatenate(vectors)
    got = lax.ppermute(packed, "y_hi", SWAP)
    low = jnp.where(shard == 0, packed, got).astype(F32)
    high = jnp.where(shard == 0, got, packed).astype(F32)
    whole, at = [], 0
    for vector in vectors:
        size = vector.shape[0]
        whole.append(jnp.concatenate([low[at : at + size], high[at : at + size]])[None])
        at += size
    c_qv, c_out, c_down, g_one, s_one, g_two, s_two, c_up = whole
    qkv = fetch(w_qkv, core)
    out = fetch(w_out, core)
    up = fetch(w_up, core)
    down = fetch(w_down, core)
    ANY = pl.BlockSpec(memory_space=pl.ANY)
    dma = pltpu.SemaphoreType.DMA
    pairs = width // (2 * HEAD_DIM)

    normed, queries, keys, values, attended, log_total = call(
        forward_attention,
        [((2 * rows, width), BF16), ((rows, width), BF16), ((2 * rows, width), BF16),
         ((2 * rows, width), BF16), ((rows, width), BF16), ((pairs, 2 * rows), F32)],
        12 * 10**9, 8 * 10**6,
        [SM, VM, VM, ANY, ANY, ANY, VM, VM, VM],
        [pltpu.VMEM((width, 3 * width), BF16), dma((3,))],
    )(place, x_prev, tokens, *qkv, c_qv, g_one, s_one)

    middle, normed_two, hidden, activated, grad_wd, grad_bd = call(
        forward_middle,
        [((rows, width), F32), ((rows, width), BF16), ((rows, ff), F32), ((rows, ff), BF16),
         ((2, 2, ff // 4, width), BF16), ((1, width), F32)],
        12 * 10**9, 16 * 10**6,
        [SM, VM, VM, ANY, ANY, ANY, VM, VM, VM, ANY, ANY, ANY, VM, VM],
        [pltpu.VMEM((width, width), BF16), pltpu.VMEM((width, ff), BF16), dma((6,))],
    )(place, attended, tokens, *out, c_out, g_two, s_two, *up, c_up, cotangent)

    chips = 1
    for axis in CHIPS:
        chips *= lax.axis_size(axis)
    copies = chips // 2
    wide, tall = width // 2, width // 2 // (copies // 4)
    down_sum = reduce_chunks(grad_wd.reshape(2, chips, ff // 4 // copies, width))
    up_shape = (2, 2, copies // 4, 4, tall, wide)

    result, grad_hidden, grad_wu, grad_bu = call(
        middle_back,
        [((rows, width), BF16), ((rows, ff), BF16), (up_shape, BF16), ((1, ff), F32)],
        12 * 10**9, 16 * 10**6,
        [SM, VM, VM, VM, VM, VM, ANY, ANY, ANY, VM],
        [pltpu.VMEM((ff, width), BF16), dma((3,))],
    )(place, cotangent, hidden, activated, normed_two, middle, *down, c_down)
    up_sum = reduce_chunks(grad_wu.reshape(2, chips, tall, wide))

    input_grad, prev_grad, grad_wa, small = call(
        input_back,
        [((rows, width), F32), ((rows, width), BF16), (up_shape, BF16), ((8, width), F32)],
        20 * 10**9, 20 * 10**6,
        [SM] + [VM] * 13 + [ANY] * 9,
        [pltpu.VMEM((rows, width), BF16), pltpu.VMEM((2 * rows, 3 * width), BF16),
         pltpu.VMEM((width, ff), BF16), pltpu.VMEM((width, width), BF16),
         pltpu.VMEM((width, 3 * width), BF16), dma((9,))],
    )(place, x_prev, tokens, cotangent, middle, grad_hidden, g_two, attended, normed, queries,
      keys, values, log_total, g_one, *up, *out, *qkv)
    attn_sum = reduce_chunks(grad_wa.reshape(2, chips, tall, wide))
    input_grad = input_grad + lax.ppermute(prev_grad, "y_hi", [(1, 0)]).astype(F32)

    small = jnp.concatenate([small[:7], grad_bd, grad_bu.reshape(ff // width, width)], axis=0)
    small = lax.psum(small, CHIPS + ("core",))

    total_wd = ordered(core, *gather_chunks(down_sum)).reshape(ff // 2, width)

    def columns(chunk):
        both = ordered(core, *gather_chunks(chunk)).reshape(2, copies // 4, 4, tall, wide)
        return jnp.transpose(both, (1, 3, 0, 2, 4)).reshape(width // 2, ff)

    total_wu = columns(up_sum)
    total_wa = columns(attn_sum)

    def mine(vector):
        size = vector.shape[0] // 2
        return lax.dynamic_slice_in_dim(vector, shard * size, size, 0)

    return (
        result,
        input_grad,
        total_wa[:, : 3 * width],
        mine(small[:2].reshape(-1)),
        total_wa[:, 3 * width :],
        mine(small[6]),
        total_wu,
        mine(small[8:].reshape(-1)),
        total_wd,
        mine(small[7]),
        mine(small[2]),
        mine(small[3]),
        mine(small[4]),
        mine(small[5]),
    )


def solution(mesh):
    axes = ("x", "z", "y_lo", "core", "y_hi")
    fine = Mesh(mesh.devices.reshape(4, 4, 2, 2, 2), axes)
    split = P(axes, None)
    matrix, vector = P("y_hi", None), P("y_hi")
    params = (matrix, vector, matrix, vector, matrix, vector, matrix, vector) + (vector,) * 4
    return jax.shard_map(
        on_device,
        mesh=fine,
        in_specs=(split,) + params + (split,),
        out_specs=(split, split) + params,
        check_vma=False,
    )
```

```python
import functools
import jax
import jax.numpy as jnp
from jax import lax
from jax.experimental import pallas as pl
from jax.experimental.pallas import tpu as pltpu
from jax.sharding import Mesh
from jax.sharding import PartitionSpec as P

HEAD_DIM = 64
eps = 1e-05
F32 = jnp.float32
BF16 = jnp.bfloat16
VMEM_LIMIT = 56 * 1024 * 1024


def dot_nn(left, right):
    return lax.dot_general(left, right, (((1,), (0,)), ((), ())), preferred_element_type=F32)


def dot_nt(left, right):
    return lax.dot_general(left, right, (((1,), (1,)), ((), ())), preferred_element_type=F32)


def dot_tn(left, right):
    return lax.dot_general(left, right, (((0,), (0,)), ((), ())), preferred_element_type=F32)


def normalise(values):
    center = jnp.mean(values, axis=-1, keepdims=True)
    centered = values - center
    spread = jnp.mean(centered * centered, axis=-1, keepdims=True)
    scale = lax.rsqrt(spread + eps)
    return centered * scale, scale


def norm_back(unit, scale, upstream, gain):
    q = upstream * gain
    return scale * (
        q
        - jnp.mean(q, axis=-1, keepdims=True)
        - unit * jnp.mean(q * unit, axis=-1, keepdims=True)
    )


def column_sum(values):
    return jnp.sum(values, axis=0, keepdims=True)


def two_heads(block):
    lane = lax.broadcasted_iota(jnp.int32, block.shape, 1)
    zero = jnp.zeros_like(block)
    return jnp.concatenate(
        [jnp.where(lane < HEAD_DIM, block, zero), jnp.where(lane < HEAD_DIM, zero, block)], axis=0
    )


def merge_heads(rows_t, count):
    row = lax.broadcasted_iota(jnp.int32, (2 * HEAD_DIM, count), 0)
    return jnp.transpose(
        jnp.where(row < HEAD_DIM, rows_t[:, :count], rows_t[:, count:]), (1, 0)
    )


def masked_scores(keys_two, queries_two, hidden_prev, count):
    scores = dot_nt(keys_two, queries_two)
    key = lax.broadcasted_iota(jnp.int32, (count, 2 * count), 0)
    query = lax.broadcasted_iota(jnp.int32, (count, 2 * count), 1)
    query = jnp.where(query >= count, query - count, query)
    prev = scores[:count] + hidden_prev
    here = jnp.where(key <= query, scores[count:], -1e30)
    return jnp.concatenate([prev, here], axis=0)


def assemble(place, parts, target, sems, first, weight=None, column=0):
    own = parts[0]
    half = own.shape[0]
    shard, core = place[0], place[1]
    quarter = half // 2
    away = (1 - shard) * half
    at = pl.multiple_of(shard * half, half)
    pieces = [(own, target.at[pl.ds(at, half)])]
    starts = (away + core * quarter, away + (1 - core) * quarter)
    for part, start in zip(parts[1:], starts):
        start = pl.multiple_of(start, quarter)
        if weight is None:
            part = part.at[:, column : column + target.shape[1]]
            pieces.append((part, target.at[pl.ds(start, quarter)]))
            continue
        outer, inner, _, tall, wide = part.shape
        for a in range(outer):
            for b in range(inner):
                row = b if weight == 0 else a * inner + b
                rows = pl.ds(pl.multiple_of(start + row * tall, tall), tall)
                left = a * wide if weight == 0 else 0
                pieces.append((part.at[a, b, weight], target.at[rows, left : left + wide]))
    copies = []
    for source, there in pieces:
        copies.append(pltpu.make_async_copy(source, there, sems.at[first + len(copies)]))
        copies[-1].start()
    return copies


def finish(copies):
    for copy in copies:
        copy.wait()


def store_rows(halves, chunk, value):
    _, across, _, along, tall, wide = halves.shape
    value = value.astype(BF16)
    for half in range(2):
        block = value[:, half * wide : (half + 1) * wide].reshape(across, along, tall, wide)
        halves[half, :, chunk] = block


def store_columns(halves, chunk, value, z_first):
    owners, rows, blocks = halves.shape[1:4]
    if z_first:
        blocks, owners, rows = owners, rows, blocks
    tall, wide = halves.shape[4:]
    value = value.astype(BF16)
    for part in range(value.shape[1] // wide):
        column = chunk * (value.shape[1] // wide) + part
        half, block = divmod(column, blocks)
        piece = value[:, part * wide : (part + 1) * wide].reshape(owners, rows, tall, wide)
        if z_first:
            halves[half, block] = piece
        else:
            halves[half, :, :, block] = piece


def hand_out(halves, core, keep, send, sems):
    copies = [
        pltpu.make_async_copy(halves.at[core], keep, sems.at[0]),
        pltpu.make_async_copy(halves.at[1 - core], send, sems.at[1]),
    ]
    for copy in copies:
        copy.start()
    return copies


def forward_attention(
    place, x_prev, x_here, own, near, far, b_qv, gain, shift,
    normed, queries, keys, values, attended, log_total, w_qkv, sems,
):
    copies = assemble(place, (own, near, far), w_qkv, sems, 0)
    rows, width = x_here.shape
    hidden_prev = jnp.where(place[0] > 0, 0.0, -1e30).astype(F32)
    for part, source in enumerate((x_prev, x_here)):
        unit, _ = normalise(source[...].astype(F32))
        normed[part * rows : (part + 1) * rows, :] = (unit * gain[...] + shift[...]).astype(BF16)
    finish(copies)
    here = normed[rows:, :]
    queries[...] = ((dot_nn(here, w_qkv[:, :width]) + b_qv[:, :width]) * 0.125).astype(BF16)
    keys[...] = dot_nn(normed[...], w_qkv[:, width : 2 * width]).astype(BF16)
    values[...] = (dot_nn(normed[...], w_qkv[:, 2 * width :]) + b_qv[:, width:]).astype(BF16)
    for pair in range(width // (2 * HEAD_DIM)):
        at = slice(pair * 2 * HEAD_DIM, (pair + 1) * 2 * HEAD_DIM)
        scores = masked_scores(keys[:, at], two_heads(queries[:, at]), hidden_prev, rows)
        top = jnp.max(scores, axis=0, keepdims=True)
        expo = jnp.exp(scores - top)
        total = jnp.sum(expo, axis=0, keepdims=True)
        probs_low = (expo * (1.0 / total)).astype(BF16)
        log_total[pair : pair + 1, :] = top + jnp.log(total)
        attended[:, at] = merge_heads(dot_tn(values[:, at], probs_low), rows).astype(BF16)


def forward_middle(
    place, attended, x_here, out_own, out_near, out_far, b_out, gain, shift,
    up_own, cells_near, cells_far, b_up, cotangent,
    middle, normed, hidden, activated, grad_w_keep, grad_w_send, grad_b_down, w_out, w_up, sems, halves, out_sems,
):
    out_copies = assemble(place, (out_own, out_near, out_far), w_out, sems, 0, column=3 * w_out.shape[0])
    up_copies = assemble(place, (up_own, cells_near, cells_far), w_up, sems, 3, 0)
    finish(out_copies)
    rows, width = x_here.shape
    mid = x_here[...].astype(F32) + (dot_nn(attended[...], w_out[...]) + b_out[...])
    middle[...] = mid
    unit, _ = normalise(mid)
    normed[...] = (unit * gain[...] + shift[...]).astype(BF16)
    finish(up_copies)
    for chunk in range(w_up.shape[1] // width):
        at = slice(chunk * width, (chunk + 1) * width)
        hid = dot_nn(normed[...], w_up[:, at]) + b_up[:, at]
        hidden[:, at] = hid
        low = jax.nn.gelu(hid, approximate=True).astype(BF16)
        activated[:, at] = low
        store_rows(halves, chunk, dot_tn(low, cotangent[...]))
    copies = hand_out(halves, place[1], grad_w_keep, grad_w_send, out_sems)
    grad_b_down[...] = column_sum(cotangent[...].astype(F32))
    finish(copies)


def gelu_slope(u):
    c = 0.7978845608028654
    t = jnp.tanh(c * (u + 0.044715 * (u * u * u)))
    return 0.5 * (1.0 + t) + 0.5 * u * (1.0 - t * t) * (c * (1.0 + 3.0 * 0.044715 * (u * u)))


def middle_back(
    place, cotangent, hidden, activated, normed, middle, own, near, far, b_down,
    result, grad_hidden, grad_w_keep, grad_w_send, grad_b_up, w_down, sems, halves, out_sems,
):
    finish(assemble(place, (own, near, far), w_down, sems, 0, 1))
    rows, width = middle.shape
    ct = cotangent[...]
    for chunk in range(w_down.shape[0] // width):
        at = slice(chunk * width, (chunk + 1) * width)
        grad_act = dot_nt(ct, w_down[at, :])
        grad_hid = (grad_act * gelu_slope(hidden[:, at])).astype(BF16)
        grad_hidden[:, at] = grad_hid
        grad_b_up[:, at] = column_sum(grad_hid.astype(F32))
        store_columns(halves, chunk, dot_tn(normed[...], grad_hid), True)
    copies = hand_out(halves, place[1], grad_w_keep, grad_w_send, out_sems)
    out = dot_nn(activated[...], w_down[...])
    result[...] = (middle[...] + (out + b_down[...])).astype(result.dtype)
    finish(copies)


def branch_back(
    place, cotangent, middle, grad_hidden, gain_two, attended,
    up_own, cells_near, cells_far, out_own, out_near, out_far,
    grad_mid, grad_att, grad_w_out, small,
    w_up, w_out, sems,
):
    up_copies = assemble(place, (up_own, cells_near, cells_far), w_up, sems, 3, 0)
    out_copies = assemble(place, (out_own, out_near, out_far), w_out, sems, 0, column=3 * w_out.shape[0])
    unit, scale = normalise(middle[...])
    finish(up_copies)
    grad_norm = dot_nt(grad_hidden[...], w_up[...])
    small[0:1, :] = column_sum(grad_norm * unit)
    small[1:2, :] = column_sum(grad_norm)
    grad = cotangent[...].astype(F32) + norm_back(unit, scale, grad_norm, gain_two[...])
    grad_mid[...] = grad
    grad_branch = grad.astype(BF16)
    small[2:3, :] = column_sum(grad_branch.astype(F32))
    small[3:8, :] = jnp.zeros((5, small.shape[1]), F32)
    finish(out_copies)
    grad_att[...] = dot_nt(grad_branch, w_out[...]).astype(BF16)
    grad_w_out[...] = dot_tn(attended[...], grad_branch).astype(BF16)


def input_back(
    place, x_prev, x_here, grad_mid, grad_att, grad_w_out, normed, queries, keys, values,
    log_total, gain_one, small, grad_b_down, grad_b_up, qkv_own, qkv_near, qkv_far,
    input_grad, prev_grad, grad_w_keep, grad_w_send, packed_keep, packed_send,
    grad_proj, w_qkv, sems, halves, out_sems,
):
    rows, width = x_here.shape
    qkv_copies = assemble(place, (qkv_own, qkv_near, qkv_far), w_qkv, sems, 0)
    hidden_prev = jnp.where(place[0] > 0, 0.0, -1e30).astype(F32)
    store_columns(halves, 3, grad_w_out[...], False)
    grad_proj[:rows, :width] = jnp.zeros((rows, width), BF16)
    for pair in range(width // (2 * HEAD_DIM)):
        at = slice(pair * 2 * HEAD_DIM, (pair + 1) * 2 * HEAD_DIM)
        queries_two = two_heads(queries[:, at])
        grads_two = two_heads(grad_att[:, at])
        scores = masked_scores(keys[:, at], queries_two, hidden_prev, rows)
        probs = jnp.exp(scores - log_total[pair : pair + 1, :])
        probs_low = probs.astype(BF16)
        grad_probs = dot_nt(values[:, at], grads_two)
        inner = jnp.sum(probs * grad_probs, axis=0, keepdims=True)
        grad_scores = (probs * (grad_probs - inner)).astype(BF16)
        first, last = pair * 2 * HEAD_DIM, (pair + 1) * 2 * HEAD_DIM
        grad_queries = merge_heads(dot_tn(keys[:, at], grad_scores), rows)
        grad_proj[rows:, at] = (grad_queries.astype(BF16) * 0.125).astype(BF16)
        grad_proj[:, width + first : width + last] = dot_nn(grad_scores, queries_two).astype(BF16)
        grad_proj[:, 2 * width + first : 2 * width + last] = dot_nn(probs_low, grads_two).astype(BF16)
    for chunk in range(3):
        at = slice(chunk * width, (chunk + 1) * width)
        store_columns(halves, chunk, dot_tn(normed[...], grad_proj[:, at]), False)
    copies = hand_out(halves, place[1], grad_w_keep, grad_w_send, out_sems)
    b_query = column_sum(grad_proj[:, :width].astype(F32))
    b_value = column_sum(grad_proj[:, 2 * width :].astype(F32))
    gain_sum = jnp.zeros((1, width), F32)
    shift_sum = jnp.zeros((1, width), F32)
    finish(qkv_copies)
    for part, source in enumerate((x_prev, x_here)):
        at = slice(part * rows, (part + 1) * rows)
        first = (1 - part) * width
        grad_norm = dot_nt(grad_proj[at, first:], w_qkv[:, first:])
        unit, scale = normalise(source[...].astype(F32))
        gain_sum = gain_sum + column_sum(grad_norm * unit)
        shift_sum = shift_sum + column_sum(grad_norm)
        grad_in = norm_back(unit, scale, grad_norm, gain_one[...])
        if part == 0:
            prev_grad[...] = grad_in.astype(prev_grad.dtype)
        else:
            input_grad[...] = grad_mid[...] + grad_in
    part = width // 2
    shared = (small[2:3, :], grad_b_down[...], gain_sum, shift_sum, small[0:1, :], small[1:2, :])
    for owner, bias in enumerate((b_query, b_value)):
        at = slice(owner * part, (owner + 1) * part)
        rows_of = [bias[:, :part], bias[:, part:]]
        rows_of += [vector[:, at] for vector in shared]
        first = owner * 4 * part
        rows_of += [grad_b_up[:, first + k * part : first + (k + 1) * part] for k in range(4)]
        zeros = jnp.zeros((2, part), F32)
        blocks = [
            jnp.concatenate(rows_of[6 * half : 6 * half + 6] + [zeros], axis=0)
            for half in range(2)
        ]
        mine = place[1] == 0
        packed_keep[owner] = jnp.where(mine, blocks[0], blocks[1])
        packed_send[owner] = jnp.where(mine, blocks[1], blocks[0])
    finish(copies)


VM = pl.BlockSpec(memory_space=pltpu.VMEM)
SM = pl.BlockSpec(memory_space=pltpu.SMEM)
ANY = pl.BlockSpec(memory_space=pl.ANY)


def call(body, outs, flops, moved, in_specs, scratch=(), away=()):
    return pl.pallas_call(
        body,
        out_shape=tuple(jax.ShapeDtypeStruct(s, d) for s, d in outs),
        in_specs=in_specs,
        out_specs=tuple(ANY if k in away else VM for k in range(len(outs))),
        scratch_shapes=list(scratch),
        compiler_params=pltpu.CompilerParams(vmem_limit_bytes=VMEM_LIMIT),
        cost_estimate=pl.CostEstimate(flops=flops, bytes_accessed=moved, transcendentals=0),
    )


Y = ("y_hi", "y_lo")
COPIES = ("y_lo", "x", "z")
PLANE = ("z", "x")
SWAP = [(0, 1), (1, 0)]


def span(axes):
    count = 1
    for axis in axes:
        count *= lax.axis_size(axis)
    return count


def after(value, *tokens):
    def body(*refs):
        pass

    return pl.pallas_call(
        body,
        out_shape=jax.ShapeDtypeStruct(value.shape, value.dtype),
        in_specs=[ANY] * (1 + len(tokens)),
        out_specs=ANY,
        input_output_aliases={0: 0},
    )(value, *tokens)


def swapped(value):
    return lax.ppermute(value, "core", SWAP)


def move(value, axes, perm):
    if axes != Y:
        return lax.ppermute(value, axes, perm)
    outer, inner = lax.axis_size(Y[0]), lax.axis_size(Y[1])

    def flat(i):
        return i % inner * outer + i // inner

    return lax.ppermute(value, Y[::-1], [(flat(a), flat(b)) for a, b in perm])


def across(value):
    count = span(Y)
    return move(value, Y, [(i, count - 1 - i) for i in range(count)])


def copied(value, axes):
    copies = span(axes)
    return lax.all_to_all(
        jnp.broadcast_to(value[None], (copies,) + value.shape), axes, 0, 0, tiled=True
    )


def summed(spread):
    return jnp.sum(spread, axis=0, dtype=F32)


def core_pair(mine, other):
    return (mine.astype(F32) + other.astype(F32)).astype(BF16)


def spread_sum(value, axes, tall, *tokens):
    chunks = value.reshape((span(axes), tall, value.shape[-1]))
    chunks = lax.all_to_all(chunks, axes, 0, 0, tiled=True)
    if tokens:
        chunks = after(chunks, *tokens)
    return summed(chunks).astype(BF16)


def finish_pair(place, mine, other, down, up):
    blocks, tall, wide = mine.shape[0], mine.shape[3], mine.shape[4]
    for half in range(2):
        keep = place[1] == half
        for block in range(blocks):
            value = jnp.where(keep, mine[block, 0, 0], other[block, 0, 0]).astype(F32)
            down[block * tall : (block + 1) * tall, half * wide : (half + 1) * wide] = value
            value = jnp.where(keep, mine[block, 0, 1], other[block, 0, 1]).astype(F32)
            start = (half * blocks + block) * wide
            up[:, start : start + wide] = value


def finish_last(place, mine, other, _, qkv, out):
    blocks, wide = mine.shape[0], mine.shape[2]
    for half in range(2):
        for block in range(blocks):
            value = jnp.where(place[1] == half, mine[block], other[block]).astype(F32)
            start = (half * blocks + block) * wide
            if start < qkv.shape[1]:
                qkv[:, start : start + wide] = value
            else:
                out[:, start - qkv.shape[1] : start - qkv.shape[1] + wide] = value


def finish_small(place, small, small_other, b_qv, b_up, *rest):
    wide = small.shape[1]
    flag = place[1] == 0
    first = jnp.where(flag, small[...], small_other[...])
    last = jnp.where(flag, small_other[...], small[...])
    rows = [first[k] for k in range(6)] + [last[k] for k in range(6)]
    for k in range(2):
        b_qv[k * wide : (k + 1) * wide] = rows[k]
    for k in range(4):
        b_up[k * wide : (k + 1) * wide] = rows[8 + k]
    for k, target in enumerate(rest):
        target[...] = rows[2 + k]


def on_device(
    tokens, w_qkv, b_qv, w_out, b_out, w_up, b_up, w_down, b_down,
    gain_one, shift_one, gain_two, shift_two, cotangent,
):
    rows, width = tokens.shape
    ff = w_up.shape[1]
    shard = lax.axis_index("y_hi")
    core = lax.axis_index("core")
    cell = lax.axis_index(PLANE)
    place = jnp.stack([shard, core]).astype(jnp.int32)
    plane, copies = span(PLANE), span(COPIES)

    half = w_qkv.shape[0] // 2
    nz, nx = lax.axis_size("z"), lax.axis_size("x")
    tall, wide = half // nx, ff // nz
    x, z = lax.axis_index("x"), lax.axis_index("z")
    first = core * half + x * tall
    up_cell = lax.dynamic_slice(w_up, (first, z * wide), (tall, wide))
    down_tall = ff // 4 // plane
    down_cell = lax.dynamic_slice_in_dim(
        w_down, core * (ff // 4) + cell * down_tall, down_tall, 0
    )
    cells = across(jnp.stack([up_cell, down_cell]))
    attn_near = [lax.dynamic_slice_in_dim(w, core * half, half, 0) for w in (w_qkv, w_out)]
    x_prev = lax.ppermute(tokens, "y_hi", [(0, 1)])
    attn_near = across(after(jnp.concatenate(attn_near, axis=1), cells, x_prev))
    vectors = (b_qv, b_out, b_down, gain_one, shift_one, gain_two, shift_two, b_up)
    length = sum(vector.shape[0] for vector in vectors)
    packed, at = jnp.zeros((length,), F32), 0
    for vector in vectors:
        end = at + vector.shape[0]
        packed = packed + jnp.pad(vector.astype(F32), (at, length - end))
        at = end
    got = lax.ppermute(packed, "y_hi", SWAP)
    cells = copied(cells, PLANE)
    cells = cells.reshape((nz, nx) + cells.shape[1:])
    attn_far = swapped(attn_near)
    qkv = (w_qkv, attn_near, attn_far)
    out = (w_out, attn_near, attn_far)

    low = jnp.where(shard == 0, packed, got)
    high = jnp.where(shard == 0, got, packed)
    whole, at = [], 0
    for vector in vectors:
        size = vector.shape[0]
        whole.append(jnp.concatenate([low[at : at + size], high[at : at + size]])[None])
        at += size
    c_qv, c_out, c_down, g_one, s_one, g_two, s_two, c_up = whole
    dma = pltpu.SemaphoreType.DMA
    pairs = width // (2 * HEAD_DIM)

    normed, queries, keys, values, attended, log_total = call(
        forward_attention,
        [((2 * rows, width), BF16), ((rows, width), BF16), ((2 * rows, width), BF16),
         ((2 * rows, width), BF16), ((rows, width), BF16), ((pairs, 2 * rows), F32)],
        9 * 10**9, 8 * 10**6,
        [SM, VM, VM, ANY, ANY, ANY, VM, VM, VM],
        [pltpu.VMEM((width, 3 * width), BF16), dma((3,))],
    )(place, x_prev, tokens, *qkv, c_qv, g_one, s_one)

    cells = after(cells, attended)
    cells_far = swapped(cells)
    up = (w_up, cells, cells_far)
    down = (w_down, cells, cells_far)
    wide, tall = width // 2, width // 2 // (copies // 4)
    down_shape = (nx, span(Y), nz, tall, wide)
    middle, normed_two, hidden, activated, keep, send, grad_bd = call(
        forward_middle,
        [((rows, width), F32), ((rows, width), BF16), ((rows, ff), F32), ((rows, ff), BF16),
         (down_shape, BF16), (down_shape, BF16), ((1, width), F32)],
        12 * 10**9, 10**5,
        [SM, VM, VM, ANY, ANY, ANY, VM, VM, VM, ANY, ANY, ANY, VM, VM],
        [pltpu.VMEM((width, width), BF16), pltpu.VMEM((width, ff), BF16), dma((4 + 2 * plane,)),
         pltpu.VMEM((2,) + down_shape, BF16), dma((2,))],
        (4, 5),
    )(place, attended, tokens, *out, c_out, g_two, s_two, *up, c_up, cotangent)

    down_both = core_pair(keep, swapped(send)).reshape(-1, wide)
    down_part = lax.psum_scatter(down_both, "x", scatter_dimension=0, tiled=True)
    up_shape = (nz, 2, copies // 4, tall, wide)
    attn_shape = (2, copies // 4, nz, tall, wide)
    activated = after(activated, down_both)

    result, grad_hidden, keep, send, grad_bu = call(
        middle_back,
        [((rows, width), BF16), ((rows, ff), BF16), (up_shape, BF16), (up_shape, BF16),
         ((1, ff), F32)],
        13 * 10**9, 10**5,
        [SM, VM, VM, VM, VM, VM, ANY, ANY, ANY, VM],
        [pltpu.VMEM((ff, width), BF16), dma((1 + 2 * plane,)), pltpu.VMEM((2,) + up_shape, BF16), dma((2,))],
        (2, 3),
    )(place, cotangent, hidden, activated, normed_two, middle, *down, c_down)

    up_both = core_pair(keep, swapped(send)).reshape(-1, wide)
    up_part = lax.psum_scatter(up_both, "z", scatter_dimension=0, tiled=True)
    grad_hidden = after(grad_hidden, up_both)

    grad_mid, grad_att, grad_wo, small = call(
        branch_back,
        [((rows, width), F32), ((rows, width), BF16), ((width, width), BF16), ((8, width), F32)],
        9 * 10**9, 10**5,
        [SM] + [VM] * 5 + [ANY] * 6,
        [pltpu.VMEM((width, ff), BF16), pltpu.VMEM((width, width), BF16), dma((4 + 2 * plane,))],
    )(place, cotangent, middle, grad_hidden, g_two, attended, *up, *out)

    down_part = after(down_part, grad_wo)
    down_sum = spread_sum(down_part, Y + ("z",), tall)
    grad_att = after(grad_att, down_part)

    input_grad, prev_grad, keep, send, small, small_send = call(
        input_back,
        [((rows, width), F32), ((rows, width), BF16), (attn_shape, BF16), (attn_shape, BF16),
         ((2, 8, wide), F32), ((2, 8, wide), F32)],
        14 * 10**9, 10**5,
        [SM] + [VM] * 14 + [ANY] * 3,
        [pltpu.VMEM((2 * rows, 3 * width), BF16), pltpu.VMEM((width, 3 * width), BF16), dma((3,)),
         pltpu.VMEM((2,) + attn_shape, BF16), dma((2,))],
        (2, 3),
    )(place, x_prev, tokens, grad_mid, grad_att, grad_wo, normed, queries, keys, values,
      log_total, g_one, small, grad_bd, grad_bu, *qkv)

    chunks = (2 * copies, tall, wide)
    attn_both = core_pair(keep, swapped(after(send, down_sum))).reshape(chunks)
    small = core_pair(small, swapped(small_send))
    small = jnp.broadcast_to(small[:, None], (2, copies) + small.shape[1:])
    attn_both = jnp.concatenate([attn_both, small.reshape((2 * copies,) + small.shape[2:])], axis=1)
    returned = lax.ppermute(prev_grad, "y_hi", [(1, 0)])
    up_part = after(up_part, down_sum, prev_grad)
    up_sum = spread_sum(up_part, Y + ("x",), tall, attn_both, returned)
    attn_both = after(attn_both, up_sum)
    attn_sum = summed(lax.all_to_all(attn_both, Y + ("x", "z"), 0, 0, tiled=True))
    attn_sum, small = attn_sum[:tall].astype(BF16), attn_sum[tall:]
    other_small = swapped(small)
    input_grad = input_grad + returned.astype(F32)
    sizes = [width, ff // 2] + [wide] * 6
    t_qv, t_up, t_out, t_down, t_g1, t_s1, t_g2, t_s2 = call(
        finish_small, [((size,), F32) for size in sizes], 10**5, 10**5, [SM, VM, VM]
    )(place, small, other_small)
    attn_mine = copied(after(attn_sum, t_qv, input_grad), COPIES)
    attn_other = swapped(attn_mine)

    pair = jnp.stack([down_sum, up_sum])
    other = lax.ppermute(pair, "y_lo", SWAP)
    low_y = lax.axis_index("y_lo") == 0
    pair = jnp.stack([jnp.where(low_y, pair, other), jnp.where(low_y, other, pair)])
    pair = lax.all_gather(pair.reshape(-1, wide), ("x", "z"), axis=0, tiled=True)
    pair = after(pair, attn_mine)
    pair = pair.reshape(plane, 2, 2, tall, wide)
    steps = copies // nz
    params = pltpu.CompilerParams(vmem_limit_bytes=VMEM_LIMIT)
    block = pl.BlockSpec((nz, 1, 2, tall, wide), lambda i: (i % nx, i // nx, 0, 0, 0))
    total_wd, total_wu = pl.pallas_call(
        finish_pair,
        grid=(steps,),
        out_shape=(
            jax.ShapeDtypeStruct((ff // 2, width), F32),
            jax.ShapeDtypeStruct((width // 2, ff), F32),
        ),
        in_specs=[SM, block, block],
        out_specs=(
            pl.BlockSpec((nz * tall, width), lambda i: (i, 0)),
            pl.BlockSpec((tall, ff), lambda i: (i, 0)),
        ),
        compiler_params=params,
        cost_estimate=pl.CostEstimate(flops=8 * 10**9, bytes_accessed=10**5, transcendentals=0),
    )(place, pair, swapped(pair))
    block = pl.BlockSpec((nz, tall, wide), lambda i: (i, 0, 0))
    total_wqkv, total_wout = pl.pallas_call(
        finish_last,
        grid=(steps,),
        out_shape=(
            jax.ShapeDtypeStruct((width // 2, 3 * width), F32),
            jax.ShapeDtypeStruct((width // 2, width), F32),
        ),
        in_specs=[SM, block, block, ANY],
        out_specs=(
            pl.BlockSpec((tall, 3 * width), lambda i: (i, 0)),
            pl.BlockSpec((tall, width), lambda i: (i, 0)),
        ),
        compiler_params=params,
        cost_estimate=pl.CostEstimate(flops=6 * 10**9, bytes_accessed=10**5, transcendentals=0),
    )(place, attn_mine, attn_other, total_wu)
    return (
        result,
        input_grad,
        total_wqkv,
        t_qv,
        total_wout,
        t_out,
        total_wu,
        t_up,
        total_wd,
        t_down,
        t_g1,
        t_s1,
        t_g2,
        t_s2,
    )


def solution(mesh):
    axes = ("x", "z", "y_lo", "core", "y_hi")
    fine = Mesh(mesh.devices.reshape(4, 4, 2, 2, 2), axes)
    split = P(axes, None)
    matrix, vector = P("y_hi", None), P("y_hi")
    params = (matrix, vector, matrix, vector, matrix, vector, matrix, vector) + (vector,) * 4
    return jax.shard_map(
        on_device,
        mesh=fine,
        in_specs=(split,) + params + (split,),
        out_specs=(split, split) + params,
        check_vma=False,
    )
```

```python
import functools
import jax
import jax.numpy as jnp
from jax import lax
from jax.experimental import pallas as pl
from jax.experimental.pallas import tpu as pltpu
from jax.sharding import Mesh
from jax.sharding import PartitionSpec as P

HEAD_DIM = 64
eps = 1e-05
F32 = jnp.float32
BF16 = jnp.bfloat16
VMEM_LIMIT = 56 * 1024 * 1024


def dot_nn(left, right):
    return lax.dot_general(left, right, (((1,), (0,)), ((), ())), preferred_element_type=F32)


def dot_nt(left, right):
    return lax.dot_general(left, right, (((1,), (1,)), ((), ())), preferred_element_type=F32)


def dot_tn(left, right):
    return lax.dot_general(left, right, (((0,), (0,)), ((), ())), preferred_element_type=F32)


def normalise(values):
    center = jnp.mean(values, axis=-1, keepdims=True)
    centered = values - center
    spread = jnp.mean(centered * centered, axis=-1, keepdims=True)
    scale = lax.rsqrt(spread + eps)
    return centered * scale, scale


def norm_back(unit, scale, upstream, gain):
    q = upstream * gain
    return scale * (
        q
        - jnp.mean(q, axis=-1, keepdims=True)
        - unit * jnp.mean(q * unit, axis=-1, keepdims=True)
    )


def column_sum(values):
    return jnp.sum(values, axis=0, keepdims=True)


def two_heads(block):
    lane = lax.broadcasted_iota(jnp.int32, block.shape, 1)
    zero = jnp.zeros_like(block)
    return jnp.concatenate(
        [jnp.where(lane < HEAD_DIM, block, zero), jnp.where(lane < HEAD_DIM, zero, block)], axis=0
    )


def merge_heads(rows_t, count):
    row = lax.broadcasted_iota(jnp.int32, (2 * HEAD_DIM, count), 0)
    return jnp.transpose(
        jnp.where(row < HEAD_DIM, rows_t[:, :count], rows_t[:, count:]), (1, 0)
    )


def masked_scores(keys_two, queries_two, hidden_prev, count):
    scores = dot_nt(keys_two, queries_two)
    key = lax.broadcasted_iota(jnp.int32, (count, 2 * count), 0)
    query = lax.broadcasted_iota(jnp.int32, (count, 2 * count), 1)
    query = jnp.where(query >= count, query - count, query)
    prev = scores[:count] + hidden_prev
    here = jnp.where(key <= query, scores[count:], -1e30)
    return jnp.concatenate([prev, here], axis=0)


def assemble(place, parts, target, sems, first, weight=None, column=0):
    own = parts[0]
    half = own.shape[0]
    shard, core = place[0], place[1]
    quarter = half // 2
    away = (1 - shard) * half
    at = pl.multiple_of(shard * half, half)
    pieces = [(own, target.at[pl.ds(at, half)])]
    starts = (away + core * quarter, away + (1 - core) * quarter)
    for part, start in zip(parts[1:], starts):
        start = pl.multiple_of(start, quarter)
        if weight is None:
            part = part.at[:, column : column + target.shape[1]]
            pieces.append((part, target.at[pl.ds(start, quarter)]))
            continue
        outer, inner, _, tall, wide = part.shape
        for a in range(outer):
            for b in range(inner):
                row = b if weight == 0 else a * inner + b
                rows = pl.ds(pl.multiple_of(start + row * tall, tall), tall)
                left = a * wide if weight == 0 else 0
                pieces.append((part.at[a, b, weight], target.at[rows, left : left + wide]))
    copies = []
    for source, there in pieces:
        copies.append(pltpu.make_async_copy(source, there, sems.at[first + len(copies)]))
        copies[-1].start()
    return copies


def finish(copies):
    for copy in copies:
        copy.wait()


def store_rows(halves, chunk, value):
    _, across, _, along, tall, wide = halves.shape
    value = value.astype(BF16)
    for half in range(2):
        block = value[:, half * wide : (half + 1) * wide].reshape(across, along, tall, wide)
        halves[half, :, chunk] = block


def store_columns(halves, chunk, value, z_first):
    owners, rows, blocks = halves.shape[1:4]
    if z_first:
        blocks, owners, rows = owners, rows, blocks
    tall, wide = halves.shape[4:]
    value = value.astype(BF16)
    for part in range(value.shape[1] // wide):
        column = chunk * (value.shape[1] // wide) + part
        half, block = divmod(column, blocks)
        piece = value[:, part * wide : (part + 1) * wide].reshape(owners, rows, tall, wide)
        if z_first:
            halves[half, block] = piece
        else:
            halves[half, :, :, block] = piece


def hand_out(halves, core, keep, send, sems):
    copies = [
        pltpu.make_async_copy(halves.at[core], keep, sems.at[0]),
        pltpu.make_async_copy(halves.at[1 - core], send, sems.at[1]),
    ]
    for copy in copies:
        copy.start()
    return copies


def forward_attention(
    place, x_prev, x_here, own, near, far, b_qv, gain, shift,
    normed, queries, keys, values, attended, log_total, w_qkv, sems,
):
    copies = assemble(place, (own, near, far), w_qkv, sems, 0)
    rows, width = x_here.shape
    hidden_prev = jnp.where(place[0] > 0, 0.0, -1e30).astype(F32)
    for part, source in enumerate((x_prev, x_here)):
        unit, _ = normalise(source[...].astype(F32))
        normed[part * rows : (part + 1) * rows, :] = (unit * gain[...] + shift[...]).astype(BF16)
    finish(copies)
    here = normed[rows:, :]
    queries[...] = ((dot_nn(here, w_qkv[:, :width]) + b_qv[:, :width]) * 0.125).astype(BF16)
    keys[...] = dot_nn(normed[...], w_qkv[:, width : 2 * width]).astype(BF16)
    values[...] = (dot_nn(normed[...], w_qkv[:, 2 * width :]) + b_qv[:, width:]).astype(BF16)
    for pair in range(width // (2 * HEAD_DIM)):
        at = slice(pair * 2 * HEAD_DIM, (pair + 1) * 2 * HEAD_DIM)
        scores = masked_scores(keys[:, at], two_heads(queries[:, at]), hidden_prev, rows)
        top = jnp.max(scores, axis=0, keepdims=True)
        expo = jnp.exp(scores - top)
        total = jnp.sum(expo, axis=0, keepdims=True)
        probs_low = (expo * (1.0 / total)).astype(BF16)
        log_total[pair : pair + 1, :] = top + jnp.log(total)
        attended[:, at] = merge_heads(dot_tn(values[:, at], probs_low), rows).astype(BF16)


def forward_middle(
    place, attended, x_here, out_own, out_near, out_far, b_out, gain, shift,
    up_own, cells_near, cells_far, b_up, cotangent,
    middle, normed, hidden, activated, grad_w_keep, grad_w_send, grad_b_down, w_out, w_up, sems, halves, out_sems,
):
    out_copies = assemble(place, (out_own, out_near, out_far), w_out, sems, 0, column=3 * w_out.shape[0])
    up_copies = assemble(place, (up_own, cells_near, cells_far), w_up, sems, 3, 0)
    finish(out_copies)
    rows, width = x_here.shape
    mid = x_here[...].astype(F32) + (dot_nn(attended[...], w_out[...]) + b_out[...])
    middle[...] = mid
    unit, _ = normalise(mid)
    normed[...] = (unit * gain[...] + shift[...]).astype(BF16)
    finish(up_copies)
    for chunk in range(w_up.shape[1] // width):
        at = slice(chunk * width, (chunk + 1) * width)
        hid = dot_nn(normed[...], w_up[:, at]) + b_up[:, at]
        hidden[:, at] = hid
        low = jax.nn.gelu(hid, approximate=True).astype(BF16)
        activated[:, at] = low
        store_rows(halves, chunk, dot_tn(low, cotangent[...]))
    copies = hand_out(halves, place[1], grad_w_keep, grad_w_send, out_sems)
    grad_b_down[...] = column_sum(cotangent[...].astype(F32))
    finish(copies)


def gelu_slope(u):
    c = 0.7978845608028654
    t = jnp.tanh(c * (u + 0.044715 * (u * u * u)))
    return 0.5 * (1.0 + t) + 0.5 * u * (1.0 - t * t) * (c * (1.0 + 3.0 * 0.044715 * (u * u)))


def middle_back(
    place, cotangent, hidden, activated, normed, middle, own, near, far, b_down,
    result, grad_hidden, grad_w_keep, grad_w_send, grad_b_up, w_down, sems, halves, out_sems,
):
    finish(assemble(place, (own, near, far), w_down, sems, 0, 1))
    rows, width = middle.shape
    ct = cotangent[...]
    for chunk in range(w_down.shape[0] // width):
        at = slice(chunk * width, (chunk + 1) * width)
        grad_act = dot_nt(ct, w_down[at, :])
        grad_hid = (grad_act * gelu_slope(hidden[:, at])).astype(BF16)
        grad_hidden[:, at] = grad_hid
        grad_b_up[:, at] = column_sum(grad_hid.astype(F32))
        store_columns(halves, chunk, dot_tn(normed[...], grad_hid), True)
    copies = hand_out(halves, place[1], grad_w_keep, grad_w_send, out_sems)
    out = dot_nn(activated[...], w_down[...])
    result[...] = (middle[...] + (out + b_down[...])).astype(result.dtype)
    finish(copies)


def branch_back(
    place, cotangent, middle, grad_hidden, gain_two, attended,
    up_own, cells_near, cells_far, out_own, out_near, out_far,
    grad_mid, grad_att, grad_w_out, small,
    w_up, w_out, sems,
):
    up_copies = assemble(place, (up_own, cells_near, cells_far), w_up, sems, 3, 0)
    out_copies = assemble(place, (out_own, out_near, out_far), w_out, sems, 0, column=3 * w_out.shape[0])
    unit, scale = normalise(middle[...])
    finish(up_copies)
    grad_norm = dot_nt(grad_hidden[...], w_up[...])
    small[0:1, :] = column_sum(grad_norm * unit)
    small[1:2, :] = column_sum(grad_norm)
    grad = cotangent[...].astype(F32) + norm_back(unit, scale, grad_norm, gain_two[...])
    grad_mid[...] = grad
    grad_branch = grad.astype(BF16)
    small[2:3, :] = column_sum(grad_branch.astype(F32))
    small[3:8, :] = jnp.zeros((5, small.shape[1]), F32)
    finish(out_copies)
    grad_att[...] = dot_nt(grad_branch, w_out[...]).astype(BF16)
    grad_w_out[...] = dot_tn(attended[...], grad_branch).astype(BF16)


def input_back(
    place, x_prev, x_here, grad_mid, grad_att, grad_w_out, normed, queries, keys, values,
    log_total, gain_one, small, grad_b_down, grad_b_up, qkv_own, qkv_near, qkv_far,
    input_grad, prev_grad, grad_w_keep, grad_w_send, packed_keep, packed_send,
    grad_proj, w_qkv, sems, halves, out_sems,
):
    rows, width = x_here.shape
    qkv_copies = assemble(place, (qkv_own, qkv_near, qkv_far), w_qkv, sems, 0)
    hidden_prev = jnp.where(place[0] > 0, 0.0, -1e30).astype(F32)
    store_columns(halves, 3, grad_w_out[...], False)
    grad_proj[:rows, :width] = jnp.zeros((rows, width), BF16)
    for pair in range(width // (2 * HEAD_DIM)):
        at = slice(pair * 2 * HEAD_DIM, (pair + 1) * 2 * HEAD_DIM)
        queries_two = two_heads(queries[:, at])
        grads_two = two_heads(grad_att[:, at])
        scores = masked_scores(keys[:, at], queries_two, hidden_prev, rows)
        probs = jnp.exp(scores - log_total[pair : pair + 1, :])
        probs_low = probs.astype(BF16)
        grad_probs = dot_nt(values[:, at], grads_two)
        inner = jnp.sum(probs * grad_probs, axis=0, keepdims=True)
        grad_scores = (probs * (grad_probs - inner)).astype(BF16)
        first, last = pair * 2 * HEAD_DIM, (pair + 1) * 2 * HEAD_DIM
        grad_queries = merge_heads(dot_tn(keys[:, at], grad_scores), rows)
        grad_proj[rows:, at] = (grad_queries.astype(BF16) * 0.125).astype(BF16)
        grad_proj[:, width + first : width + last] = dot_nn(grad_scores, queries_two).astype(BF16)
        grad_proj[:, 2 * width + first : 2 * width + last] = dot_nn(probs_low, grads_two).astype(BF16)
    for chunk in range(3):
        at = slice(chunk * width, (chunk + 1) * width)
        store_columns(halves, chunk, dot_tn(normed[...], grad_proj[:, at]), False)
    copies = hand_out(halves, place[1], grad_w_keep, grad_w_send, out_sems)
    b_query = column_sum(grad_proj[:, :width].astype(F32))
    b_value = column_sum(grad_proj[:, 2 * width :].astype(F32))
    gain_sum = jnp.zeros((1, width), F32)
    shift_sum = jnp.zeros((1, width), F32)
    finish(qkv_copies)
    for part, source in enumerate((x_prev, x_here)):
        at = slice(part * rows, (part + 1) * rows)
        first = (1 - part) * width
        grad_norm = dot_nt(grad_proj[at, first:], w_qkv[:, first:])
        unit, scale = normalise(source[...].astype(F32))
        gain_sum = gain_sum + column_sum(grad_norm * unit)
        shift_sum = shift_sum + column_sum(grad_norm)
        grad_in = norm_back(unit, scale, grad_norm, gain_one[...])
        if part == 0:
            prev_grad[...] = grad_in.astype(prev_grad.dtype)
        else:
            input_grad[...] = grad_mid[...] + grad_in
    part = width // 2
    shared = (small[2:3, :], grad_b_down[...], gain_sum, shift_sum, small[0:1, :], small[1:2, :])
    for owner, bias in enumerate((b_query, b_value)):
        at = slice(owner * part, (owner + 1) * part)
        rows_of = [bias[:, :part], bias[:, part:]]
        rows_of += [vector[:, at] for vector in shared]
        first = owner * 4 * part
        rows_of += [grad_b_up[:, first + k * part : first + (k + 1) * part] for k in range(4)]
        zeros = jnp.zeros((2, part), F32)
        blocks = [
            jnp.concatenate(rows_of[6 * half : 6 * half + 6] + [zeros], axis=0)
            for half in range(2)
        ]
        mine = place[1] == 0
        packed_keep[owner] = jnp.where(mine, blocks[0], blocks[1])
        packed_send[owner] = jnp.where(mine, blocks[1], blocks[0])
    finish(copies)


VM = pl.BlockSpec(memory_space=pltpu.VMEM)
SM = pl.BlockSpec(memory_space=pltpu.SMEM)
ANY = pl.BlockSpec(memory_space=pl.ANY)


def call(body, outs, flops, moved, in_specs, scratch=(), away=()):
    return pl.pallas_call(
        body,
        out_shape=tuple(jax.ShapeDtypeStruct(s, d) for s, d in outs),
        in_specs=in_specs,
        out_specs=tuple(ANY if k in away else VM for k in range(len(outs))),
        scratch_shapes=list(scratch),
        compiler_params=pltpu.CompilerParams(vmem_limit_bytes=VMEM_LIMIT),
        cost_estimate=pl.CostEstimate(flops=flops, bytes_accessed=moved, transcendentals=0),
    )


Y = ("y_hi", "y_lo")
COPIES = ("y_lo", "x", "z")
PLANE = ("z", "x")
SWAP = [(0, 1), (1, 0)]


def span(axes):
    count = 1
    for axis in axes:
        count *= lax.axis_size(axis)
    return count


def after(value, *tokens):
    def body(*refs):
        pass

    return pl.pallas_call(
        body,
        out_shape=jax.ShapeDtypeStruct(value.shape, value.dtype),
        in_specs=[ANY] * (1 + len(tokens)),
        out_specs=ANY,
        input_output_aliases={0: 0},
    )(value, *tokens)


def swapped(value):
    return lax.ppermute(value, "core", SWAP)


def move(value, axes, perm):
    if axes != Y:
        return lax.ppermute(value, axes, perm)
    outer, inner = lax.axis_size(Y[0]), lax.axis_size(Y[1])

    def flat(i):
        return i % inner * outer + i // inner

    return lax.ppermute(value, Y[::-1], [(flat(a), flat(b)) for a, b in perm])


def across(value):
    count = span(Y)
    return move(value, Y, [(i, count - 1 - i) for i in range(count)])


def repeated(value, axes):
    return jnp.broadcast_to(value[None], (span(axes),) + value.shape)


def copied(value, axes):
    return lax.all_to_all(repeated(value, axes), axes, 0, 0, tiled=True)


def summed(spread):
    return jnp.sum(spread, axis=0, dtype=F32)


def core_pair(mine, other):
    return (mine.astype(F32) + other.astype(F32)).astype(BF16)


def ring_pieces(keep, other, at, axes):
    count = span(axes)
    me = lax.axis_index(axes)

    def piece(step):
        index = lax.rem(me + step, count)
        mine = lax.dynamic_index_in_dim(keep, index, at, keepdims=False)
        theirs = lax.dynamic_index_in_dim(other, index, at, keepdims=False)
        return mine.astype(F32) + theirs.astype(F32)

    return [piece(step) if step == 0 else piece(step).astype(BF16) for step in range(count)]


def ring_sum(pieces, axes, rest, received):
    count = len(pieces)
    total = pieces[0]
    for step in range(1, count):
        perm = [(i, (i + step) % count) for i in range(count)]
        total = total + received(move(pieces[step], axes, perm)).astype(F32)
    total = total.astype(BF16)
    spread = total.reshape((span(rest),) + total.shape[-2:])
    return spread


def spread(value, axes):
    chunks = value.reshape((span(axes), -1, value.shape[-1]))
    return lax.all_to_all(chunks, axes, 0, 0, tiled=True)


def finish_all(place, pair, pair_other, attn, attn_other, grad, returned, down, up, qkv, out, total):
    total[...] = grad[...] + returned[...].astype(F32)
    blocks, tall, wide = attn.shape
    for half in range(2):
        keep = place[1] == half
        for block in range(blocks):
            value = jnp.where(keep, pair[block, 0, 0], pair_other[block, 0, 0]).astype(F32)
            down[block * tall : (block + 1) * tall, half * wide : (half + 1) * wide] = value
            value = jnp.where(keep, pair[block, 0, 1], pair_other[block, 0, 1]).astype(F32)
            start = (half * blocks + block) * wide
            up[:, start : start + wide] = value
            value = jnp.where(keep, attn[block], attn_other[block]).astype(F32)
            if start < qkv.shape[1]:
                qkv[:, start : start + wide] = value
            else:
                out[:, start - qkv.shape[1] : start - qkv.shape[1] + wide] = value


def finish_small(place, small, small_other, b_qv, b_up, *rest):
    wide = small.shape[1]
    flag = place[1] == 0
    first = jnp.where(flag, small[...], small_other[...])
    last = jnp.where(flag, small_other[...], small[...])
    rows = [first[k] for k in range(6)] + [last[k] for k in range(6)]
    for k in range(2):
        b_qv[k * wide : (k + 1) * wide] = rows[k]
    for k in range(4):
        b_up[k * wide : (k + 1) * wide] = rows[8 + k]
    for k, target in enumerate(rest):
        target[...] = rows[2 + k]


def on_device(
    tokens, w_qkv, b_qv, w_out, b_out, w_up, b_up, w_down, b_down,
    gain_one, shift_one, gain_two, shift_two, cotangent,
):
    rows, width = tokens.shape
    ff = w_up.shape[1]
    shard = lax.axis_index("y_hi")
    core = lax.axis_index("core")
    cell = lax.axis_index(PLANE)
    place = jnp.stack([shard, core]).astype(jnp.int32)
    plane, copies = span(PLANE), span(COPIES)

    half = w_qkv.shape[0] // 2
    nz, nx = lax.axis_size("z"), lax.axis_size("x")
    tall, wide = half // nx, ff // nz
    x, z = lax.axis_index("x"), lax.axis_index("z")
    first = core * half + x * tall
    up_cell = lax.dynamic_slice(w_up, (first, z * wide), (tall, wide))
    down_tall = ff // 4 // plane
    down_cell = lax.dynamic_slice_in_dim(
        w_down, core * (ff // 4) + cell * down_tall, down_tall, 0
    )
    cells = across(jnp.stack([up_cell, down_cell]))
    cells = repeated(cells, PLANE)
    attn_near = [lax.dynamic_slice_in_dim(w, core * half, half, 0) for w in (w_qkv, w_out)]
    x_prev = lax.ppermute(tokens, "y_hi", [(0, 1)])
    vectors = (b_qv, b_out, b_down, gain_one, shift_one, gain_two, shift_two, b_up)
    length = sum(vector.shape[0] for vector in vectors)
    packed, at = jnp.zeros((length,), F32), 0
    for vector in vectors:
        end = at + vector.shape[0]
        packed = packed + jnp.pad(vector.astype(F32), (at, length - end))
        at = end
    got = lax.ppermute(packed, "y_hi", SWAP)
    attn_near = across(after(jnp.concatenate(attn_near, axis=1), cells, x_prev, got))
    cells = lax.all_to_all(cells, PLANE, 0, 0, tiled=True)
    cells = cells.reshape((nz, nx) + cells.shape[1:])
    attn_far = swapped(attn_near)
    qkv = (w_qkv, attn_near, attn_far)
    out = (w_out, attn_near, attn_far)

    low = jnp.where(shard == 0, packed, got)
    high = jnp.where(shard == 0, got, packed)
    whole, at = [], 0
    for vector in vectors:
        size = vector.shape[0]
        whole.append(jnp.concatenate([low[at : at + size], high[at : at + size]])[None])
        at += size
    c_qv, c_out, c_down, g_one, s_one, g_two, s_two, c_up = whole
    dma = pltpu.SemaphoreType.DMA
    pairs = width // (2 * HEAD_DIM)

    normed, queries, keys, values, attended, log_total = call(
        forward_attention,
        [((2 * rows, width), BF16), ((rows, width), BF16), ((2 * rows, width), BF16),
         ((2 * rows, width), BF16), ((rows, width), BF16), ((pairs, 2 * rows), F32)],
        9 * 10**9, 8 * 10**6,
        [SM, VM, VM, ANY, ANY, ANY, VM, VM, VM],
        [pltpu.VMEM((width, 3 * width), BF16), dma((3,))],
    )(place, x_prev, tokens, *qkv, c_qv, g_one, s_one)

    cells = after(cells, attended)
    cells_far = swapped(cells)
    up = (w_up, cells, cells_far)
    down = (w_down, cells, cells_far)
    wide, tall = width // 2, width // 2 // (copies // 4)
    down_shape = (nx, span(Y), nz, tall, wide)
    middle, normed_two, hidden, activated, keep, send, grad_bd = call(
        forward_middle,
        [((rows, width), F32), ((rows, width), BF16), ((rows, ff), F32), ((rows, ff), BF16),
         (down_shape, BF16), (down_shape, BF16), ((1, width), F32)],
        12 * 10**9, 10**5,
        [SM, VM, VM, ANY, ANY, ANY, VM, VM, VM, ANY, ANY, ANY, VM, VM],
        [pltpu.VMEM((width, width), BF16), pltpu.VMEM((width, ff), BF16), dma((4 + 2 * plane,)),
         pltpu.VMEM((2,) + down_shape, BF16), dma((2,))],
        (4, 5),
    )(place, attended, tokens, *out, c_out, g_two, s_two, *up, c_up, cotangent)

    down_both = core_pair(keep, swapped(send)).reshape(-1, wide)
    down_part = lax.psum_scatter(down_both, "x", scatter_dimension=0, tiled=True)
    up_shape = (nz, 2, copies // 4, tall, wide)
    attn_shape = (2, copies // 4, nz, tall, wide)
    activated = after(activated, down_both)

    result, grad_hidden, keep, send, grad_bu = call(
        middle_back,
        [((rows, width), BF16), ((rows, ff), BF16), (up_shape, BF16), (up_shape, BF16),
         ((1, ff), F32)],
        13 * 10**9, 10**5,
        [SM, VM, VM, VM, VM, VM, ANY, ANY, ANY, VM],
        [pltpu.VMEM((ff, width), BF16), dma((1 + 2 * plane,)), pltpu.VMEM((2,) + up_shape, BF16), dma((2,))],
        (2, 3),
    )(place, cotangent, hidden, activated, normed_two, middle, *down, c_down)

    grid = (nz, span(Y), nx, tall, wide)
    up_pieces = ring_pieces(keep.reshape(grid), swapped(send).reshape(grid), 0, "z")
    grad_hidden = after(grad_hidden, *up_pieces[1:])

    grad_mid, grad_att, grad_wo, small = call(
        branch_back,
        [((rows, width), F32), ((rows, width), BF16), ((width, width), BF16), ((8, width), F32)],
        9 * 10**9, 10**5,
        [SM] + [VM] * 5 + [ANY] * 6,
        [pltpu.VMEM((width, ff), BF16), pltpu.VMEM((width, width), BF16), dma((4 + 2 * plane,))],
    )(place, cotangent, middle, grad_hidden, g_two, attended, *up, *out)

    down_part = after(down_part, grad_wo)
    down_sum = summed(spread(down_part, Y + ("z",))).astype(BF16)
    grad_att = after(grad_att, down_part)

    input_grad, prev_grad, keep, send, small, small_send = call(
        input_back,
        [((rows, width), F32), ((rows, width), BF16), (attn_shape, BF16), (attn_shape, BF16),
         ((2, 8, wide), F32), ((2, 8, wide), F32)],
        14 * 10**9, 10**5,
        [SM] + [VM] * 14 + [ANY] * 3,
        [pltpu.VMEM((2 * rows, 3 * width), BF16), pltpu.VMEM((width, 3 * width), BF16), dma((3,)),
         pltpu.VMEM((2,) + attn_shape, BF16), dma((2,))],
        (2, 3),
    )(place, x_prev, tokens, grad_mid, grad_att, grad_wo, normed, queries, keys, values,
      log_total, g_one, small, grad_bd, grad_bu, *qkv)

    chunks = (2 * copies, tall, wide)
    up_part = ring_sum(
        up_pieces, "z", Y + ("x",), lambda value: after(value, prev_grad, grad_mid)
    )
    attn_both = core_pair(keep, swapped(after(send, down_sum, up_part))).reshape(chunks)
    small = core_pair(small, swapped(small_send))
    small = jnp.broadcast_to(small[:, None], (2, copies) + small.shape[1:])
    attn_both = jnp.concatenate([attn_both, small.reshape((2 * copies,) + small.shape[2:])], axis=1)
    returned = lax.ppermute(prev_grad, "y_hi", [(1, 0)])
    up_part = after(up_part, down_sum, prev_grad)
    up_chunks = spread(up_part, Y + ("x",))
    up_chunks = after(up_chunks, attn_both, returned)
    up_sum = summed(up_chunks).astype(BF16)
    pair = jnp.stack([down_sum, up_sum])
    other = lax.ppermute(pair, "y_lo", SWAP)
    low_y = lax.axis_index("y_lo") == 0
    pair = jnp.stack([jnp.where(low_y, pair, other), jnp.where(low_y, other, pair)])
    attn_chunks = spread(after(attn_both, up_chunks), Y + ("x", "z"))
    attn_sum = summed(after(attn_chunks, pair))
    attn_sum, small = attn_sum[:tall].astype(BF16), attn_sum[tall:]
    other_small = swapped(small)
    sizes = [width, ff // 2] + [wide] * 6
    t_qv, t_up, t_out, t_down, t_g1, t_s1, t_g2, t_s2 = call(
        finish_small, [((size,), F32) for size in sizes], 10**5, 10**5, [SM, VM, VM]
    )(place, small, other_small)
    attn_mine = copied(after(attn_sum, t_qv), COPIES)
    attn_other = swapped(attn_mine)

    pair = lax.all_gather(pair.reshape(-1, wide), ("x", "z"), axis=0, tiled=True)
    pair = after(pair, attn_mine)
    pair = pair.reshape(plane, 2, 2, tall, wide)
    steps = copies // nz
    pair_block = pl.BlockSpec((nz, 1, 2, tall, wide), lambda i: (i % nx, i // nx, 0, 0, 0))
    attn_block = pl.BlockSpec((nz, tall, wide), lambda i: (i, 0, 0))
    shapes = ((ff // 2, width), (width // 2, ff), (width // 2, 3 * width), (width // 2, width))
    shapes += ((rows, width),)
    row_blocks = [
        pl.BlockSpec((high // steps, broad), lambda i: (i, 0)) for high, broad in shapes
    ]
    total_wd, total_wu, total_wqkv, total_wout, input_grad = pl.pallas_call(
        finish_all,
        grid=(steps,),
        out_shape=tuple(jax.ShapeDtypeStruct(shape, F32) for shape in shapes),
        in_specs=[SM, pair_block, pair_block, attn_block, attn_block] + [row_blocks[-1]] * 2,
        out_specs=tuple(row_blocks),
        compiler_params=pltpu.CompilerParams(vmem_limit_bytes=VMEM_LIMIT),
        cost_estimate=pl.CostEstimate(flops=14 * 10**9, bytes_accessed=10**5, transcendentals=0),
    )(place, pair, swapped(pair), attn_mine, attn_other, input_grad, returned)
    return (
        result,
        input_grad,
        total_wqkv,
        t_qv,
        total_wout,
        t_out,
        total_wu,
        t_up,
        total_wd,
        t_down,
        t_g1,
        t_s1,
        t_g2,
        t_s2,
    )


def solution(mesh):
    axes = ("x", "z", "y_lo", "core", "y_hi")
    fine = Mesh(mesh.devices.reshape(4, 4, 2, 2, 2), axes)
    split = P(axes, None)
    matrix, vector = P("y_hi", None), P("y_hi")
    params = (matrix, vector, matrix, vector, matrix, vector, matrix, vector) + (vector,) * 4
    return jax.shard_map(
        on_device,
        mesh=fine,
        in_specs=(split,) + params + (split,),
        out_specs=(split, split) + params,
        check_vma=False,
    )
```

```python
import functools
import jax
import jax.numpy as jnp
from jax import lax
from jax.experimental import pallas as pl
from jax.experimental.pallas import tpu as pltpu
from jax.sharding import Mesh
from jax.sharding import PartitionSpec as P

HEAD_DIM = 64
eps = 1e-05
F32 = jnp.float32
BF16 = jnp.bfloat16
VMEM_LIMIT = 63 * 1024 * 1024 + 512 * 1024


def dot_nn(left, right):
    return lax.dot_general(left, right, (((1,), (0,)), ((), ())), preferred_element_type=F32)


def dot_nt(left, right):
    return lax.dot_general(left, right, (((1,), (1,)), ((), ())), preferred_element_type=F32)


def dot_tn(left, right):
    return lax.dot_general(left, right, (((0,), (0,)), ((), ())), preferred_element_type=F32)


def normalise(values):
    center = jnp.mean(values, axis=-1, keepdims=True)
    centered = values - center
    spread = jnp.mean(centered * centered, axis=-1, keepdims=True)
    scale = lax.rsqrt(spread + eps)
    return centered * scale, scale


def norm_back(unit, scale, upstream, gain):
    q = upstream * gain
    return scale * (
        q
        - jnp.mean(q, axis=-1, keepdims=True)
        - unit * jnp.mean(q * unit, axis=-1, keepdims=True)
    )


def column_sum(values):
    return jnp.sum(values, axis=0, keepdims=True)


def two_heads(block):
    lane = lax.broadcasted_iota(jnp.int32, block.shape, 1)
    zero = jnp.zeros_like(block)
    return jnp.concatenate(
        [jnp.where(lane < HEAD_DIM, block, zero), jnp.where(lane < HEAD_DIM, zero, block)], axis=0
    )


def merge_heads(rows_t, count):
    row = lax.broadcasted_iota(jnp.int32, (2 * HEAD_DIM, count), 0)
    return jnp.transpose(
        jnp.where(row < HEAD_DIM, rows_t[:, :count], rows_t[:, count:]), (1, 0)
    )


def masked_scores(keys_two, queries_two, hidden_prev, count):
    scores = dot_nt(keys_two, queries_two)
    key = lax.broadcasted_iota(jnp.int32, (count, 2 * count), 0)
    query = lax.broadcasted_iota(jnp.int32, (count, 2 * count), 1)
    query = jnp.where(query >= count, query - count, query)
    prev = scores[:count] + hidden_prev
    here = jnp.where(key <= query, scores[count:], -1e30)
    return jnp.concatenate([prev, here], axis=0)


def assemble(place, parts, target, sems, first, weight=None, column=0):
    own = parts[0]
    half = own.shape[0]
    shard, core = place[0], place[1]
    quarter = half // 2
    away = (1 - shard) * half
    at = pl.multiple_of(shard * half, half)
    pieces = [(own, target.at[pl.ds(at, half)])]
    starts = (away + core * quarter, away + (1 - core) * quarter)
    for part, start in zip(parts[1:], starts):
        start = pl.multiple_of(start, quarter)
        if weight is None:
            part = part.at[:, column : column + target.shape[1]]
            pieces.append((part, target.at[pl.ds(start, quarter)]))
            continue
        outer, inner, _, tall, wide = part.shape
        for a in range(outer):
            for b in range(inner):
                row = b if weight == 0 else a * inner + b
                rows = pl.ds(pl.multiple_of(start + row * tall, tall), tall)
                left = a * wide if weight == 0 else 0
                pieces.append((part.at[a, b, weight], target.at[rows, left : left + wide]))
    copies = []
    for source, there in pieces:
        copies.append(pltpu.make_async_copy(source, there, sems.at[first + len(copies)]))
        copies[-1].start()
    return copies


def finish(copies):
    for copy in copies:
        copy.wait()


def store_rows(halves, chunk, value):
    _, across, _, along, tall, wide = halves.shape
    value = value.astype(BF16)
    for half in range(2):
        block = value[:, half * wide : (half + 1) * wide].reshape(across, along, tall, wide)
        halves[half, :, chunk] = block


def store_columns(halves, chunk, value, z_first):
    owners, rows, blocks = halves.shape[1:4]
    if z_first:
        blocks, owners, rows = owners, rows, blocks
    tall, wide = halves.shape[4:]
    value = value.astype(BF16)
    for part in range(value.shape[1] // wide):
        column = chunk * (value.shape[1] // wide) + part
        half, block = divmod(column, blocks)
        piece = value[:, part * wide : (part + 1) * wide].reshape(owners, rows, tall, wide)
        if z_first:
            halves[half, block] = piece
        else:
            halves[half, :, :, block] = piece


def hand_out(halves, core, keep, send, sems):
    copies = [
        pltpu.make_async_copy(halves.at[core], keep, sems.at[0]),
        pltpu.make_async_copy(halves.at[1 - core], send, sems.at[1]),
    ]
    for copy in copies:
        copy.start()
    return copies


def forward_attention(
    place, x_prev, x_here, own, near, far, b_qv, gain, shift,
    normed, queries, keys, values, attended, log_total, w_qkv, sems,
):
    copies = assemble(place, (own, near, far), w_qkv, sems, 0)
    rows, width = x_here.shape
    hidden_prev = jnp.where(place[0] > 0, 0.0, -1e30).astype(F32)
    for part, source in enumerate((x_prev, x_here)):
        unit, _ = normalise(source[...].astype(F32))
        normed[part * rows : (part + 1) * rows, :] = (unit * gain[...] + shift[...]).astype(BF16)
    finish(copies)
    here = normed[rows:, :]
    queries[...] = ((dot_nn(here, w_qkv[:, :width]) + b_qv[:, :width]) * 0.125).astype(BF16)
    keys[...] = dot_nn(normed[...], w_qkv[:, width : 2 * width]).astype(BF16)
    values[...] = (dot_nn(normed[...], w_qkv[:, 2 * width :]) + b_qv[:, width:]).astype(BF16)
    for pair in range(width // (2 * HEAD_DIM)):
        at = slice(pair * 2 * HEAD_DIM, (pair + 1) * 2 * HEAD_DIM)
        scores = masked_scores(keys[:, at], two_heads(queries[:, at]), hidden_prev, rows)
        top = jnp.max(scores, axis=0, keepdims=True)
        expo = jnp.exp(scores - top)
        total = jnp.sum(expo, axis=0, keepdims=True)
        probs_low = (expo * (1.0 / total)).astype(BF16)
        log_total[pair : pair + 1, :] = top + jnp.log(total)
        attended[:, at] = merge_heads(dot_tn(values[:, at], probs_low), rows).astype(BF16)


def forward_middle(
    place, attended, x_here, out_own, out_near, out_far, b_out, gain, shift,
    up_own, cells_near, cells_far, b_up, cotangent,
    middle, normed, hidden, activated, grad_w_keep, grad_w_send, grad_b_down, w_out, w_up, sems, halves, out_sems,
):
    out_copies = assemble(place, (out_own, out_near, out_far), w_out, sems, 0, column=3 * w_out.shape[0])
    up_copies = assemble(place, (up_own, cells_near, cells_far), w_up, sems, 3, 0)
    finish(out_copies)
    rows, width = x_here.shape
    mid = x_here[...].astype(F32) + (dot_nn(attended[...], w_out[...]) + b_out[...])
    middle[...] = mid
    unit, _ = normalise(mid)
    normed[...] = (unit * gain[...] + shift[...]).astype(BF16)
    finish(up_copies)
    for chunk in range(w_up.shape[1] // width):
        at = slice(chunk * width, (chunk + 1) * width)
        hid = dot_nn(normed[...], w_up[:, at]) + b_up[:, at]
        hidden[:, at] = hid
        low = jax.nn.gelu(hid, approximate=True).astype(BF16)
        activated[:, at] = low
        store_rows(halves, chunk, dot_tn(low, cotangent[...]))
    copies = hand_out(halves, place[1], grad_w_keep, grad_w_send, out_sems)
    grad_b_down[...] = column_sum(cotangent[...].astype(F32))
    finish(copies)


def gelu_slope(u):
    c = 0.7978845608028654
    t = jnp.tanh(c * (u + 0.044715 * (u * u * u)))
    return 0.5 * (1.0 + t) + 0.5 * u * (1.0 - t * t) * (c * (1.0 + 3.0 * 0.044715 * (u * u)))


def middle_back(
    place, cotangent, hidden, activated, normed, middle, own, near, far, b_down,
    result, grad_hidden, grad_w_keep, grad_w_send, grad_b_up, w_down, sems, halves, out_sems,
):
    finish(assemble(place, (own, near, far), w_down, sems, 0, 1))
    rows, width = middle.shape
    ct = cotangent[...]
    for chunk in range(w_down.shape[0] // width):
        at = slice(chunk * width, (chunk + 1) * width)
        grad_act = dot_nt(ct, w_down[at, :])
        grad_hid = (grad_act * gelu_slope(hidden[:, at])).astype(BF16)
        grad_hidden[:, at] = grad_hid
        grad_b_up[:, at] = column_sum(grad_hid.astype(F32))
        store_columns(halves, chunk, dot_tn(normed[...], grad_hid), True)
    copies = hand_out(halves, place[1], grad_w_keep, grad_w_send, out_sems)
    out = dot_nn(activated[...], w_down[...])
    result[...] = (middle[...] + (out + b_down[...])).astype(result.dtype)
    finish(copies)


def branch_back(
    place, cotangent, middle, grad_hidden, gain_two, attended,
    up_own, cells_near, cells_far, out_own, out_near, out_far,
    grad_mid, grad_att, grad_w_out, small,
    w_up, w_out, sems,
):
    up_copies = assemble(place, (up_own, cells_near, cells_far), w_up, sems, 3, 0)
    out_copies = assemble(place, (out_own, out_near, out_far), w_out, sems, 0, column=3 * w_out.shape[0])
    unit, scale = normalise(middle[...])
    finish(up_copies)
    grad_norm = dot_nt(grad_hidden[...], w_up[...])
    small[0:1, :] = column_sum(grad_norm * unit)
    small[1:2, :] = column_sum(grad_norm)
    grad = cotangent[...].astype(F32) + norm_back(unit, scale, grad_norm, gain_two[...])
    grad_mid[...] = grad
    grad_branch = grad.astype(BF16)
    small[2:3, :] = column_sum(grad_branch.astype(F32))
    small[3:8, :] = jnp.zeros((5, small.shape[1]), F32)
    finish(out_copies)
    grad_att[...] = dot_nt(grad_branch, w_out[...]).astype(BF16)
    grad_w_out[...] = dot_tn(attended[...], grad_branch).astype(BF16)


def input_back(
    place, x_prev, x_here, grad_mid, grad_att, grad_w_out, normed, queries, keys, values,
    log_total, gain_one, small, grad_b_down, grad_b_up, qkv_own, qkv_near, qkv_far,
    input_grad, prev_grad, grad_w_keep, grad_w_send, packed_keep, packed_send,
    grad_proj, w_qkv, sems, halves, out_sems,
):
    rows, width = x_here.shape
    qkv_copies = assemble(place, (qkv_own, qkv_near, qkv_far), w_qkv, sems, 0)
    hidden_prev = jnp.where(place[0] > 0, 0.0, -1e30).astype(F32)
    store_columns(halves, 3, grad_w_out[...], False)
    grad_proj[:rows, :width] = jnp.zeros((rows, width), BF16)
    for pair in range(width // (2 * HEAD_DIM)):
        at = slice(pair * 2 * HEAD_DIM, (pair + 1) * 2 * HEAD_DIM)
        queries_two = two_heads(queries[:, at])
        grads_two = two_heads(grad_att[:, at])
        scores = masked_scores(keys[:, at], queries_two, hidden_prev, rows)
        probs = jnp.exp(scores - log_total[pair : pair + 1, :])
        probs_low = probs.astype(BF16)
        grad_probs = dot_nt(values[:, at], grads_two)
        inner = jnp.sum(probs * grad_probs, axis=0, keepdims=True)
        grad_scores = (probs * (grad_probs - inner)).astype(BF16)
        first, last = pair * 2 * HEAD_DIM, (pair + 1) * 2 * HEAD_DIM
        grad_queries = merge_heads(dot_tn(keys[:, at], grad_scores), rows)
        grad_proj[rows:, at] = (grad_queries.astype(BF16) * 0.125).astype(BF16)
        grad_proj[:, width + first : width + last] = dot_nn(grad_scores, queries_two).astype(BF16)
        grad_proj[:, 2 * width + first : 2 * width + last] = dot_nn(probs_low, grads_two).astype(BF16)
    for chunk in range(3):
        at = slice(chunk * width, (chunk + 1) * width)
        store_columns(halves, chunk, dot_tn(normed[...], grad_proj[:, at]), False)
    copies = hand_out(halves, place[1], grad_w_keep, grad_w_send, out_sems)
    b_query = column_sum(grad_proj[:, :width].astype(F32))
    b_value = column_sum(grad_proj[:, 2 * width :].astype(F32))
    gain_sum = jnp.zeros((1, width), F32)
    shift_sum = jnp.zeros((1, width), F32)
    finish(qkv_copies)
    for part, source in enumerate((x_prev, x_here)):
        at = slice(part * rows, (part + 1) * rows)
        first = (1 - part) * width
        grad_norm = dot_nt(grad_proj[at, first:], w_qkv[:, first:])
        unit, scale = normalise(source[...].astype(F32))
        gain_sum = gain_sum + column_sum(grad_norm * unit)
        shift_sum = shift_sum + column_sum(grad_norm)
        grad_in = norm_back(unit, scale, grad_norm, gain_one[...])
        if part == 0:
            prev_grad[...] = grad_in.astype(prev_grad.dtype)
        else:
            input_grad[...] = grad_mid[...] + grad_in
    part = width // 2
    shared = (small[2:3, :], grad_b_down[...], gain_sum, shift_sum, small[0:1, :], small[1:2, :])
    for owner, bias in enumerate((b_query, b_value)):
        at = slice(owner * part, (owner + 1) * part)
        rows_of = [bias[:, :part], bias[:, part:]]
        rows_of += [vector[:, at] for vector in shared]
        first = owner * 4 * part
        rows_of += [grad_b_up[:, first + k * part : first + (k + 1) * part] for k in range(4)]
        zeros = jnp.zeros((2, part), F32)
        blocks = [
            jnp.concatenate(rows_of[6 * half : 6 * half + 6] + [zeros], axis=0)
            for half in range(2)
        ]
        mine = place[1] == 0
        packed_keep[owner] = jnp.where(mine, blocks[0], blocks[1])
        packed_send[owner] = jnp.where(mine, blocks[1], blocks[0])
    finish(copies)


VM = pl.BlockSpec(memory_space=pltpu.VMEM)
SM = pl.BlockSpec(memory_space=pltpu.SMEM)
ANY = pl.BlockSpec(memory_space=pl.ANY)


def call(body, outs, flops, moved, in_specs, scratch=(), away=()):
    return pl.pallas_call(
        body,
        out_shape=tuple(jax.ShapeDtypeStruct(s, d) for s, d in outs),
        in_specs=in_specs,
        out_specs=tuple(ANY if k in away else VM for k in range(len(outs))),
        scratch_shapes=list(scratch),
        compiler_params=pltpu.CompilerParams(vmem_limit_bytes=VMEM_LIMIT),
        cost_estimate=pl.CostEstimate(flops=flops, bytes_accessed=moved, transcendentals=0),
    )


Y = ("y_hi", "y_lo")
COPIES = ("y_lo", "x", "z")
PLANE = ("z", "x")
SWAP = [(0, 1), (1, 0)]


def span(axes):
    count = 1
    for axis in axes:
        count *= lax.axis_size(axis)
    return count


def after(value, *tokens):
    def body(*refs):
        pass

    return pl.pallas_call(
        body,
        out_shape=jax.ShapeDtypeStruct(value.shape, value.dtype),
        in_specs=[ANY] * (1 + len(tokens)),
        out_specs=ANY,
        input_output_aliases={0: 0},
        compiler_params=pltpu.CompilerParams(vmem_limit_bytes=VMEM_LIMIT),
    )(value, *tokens)


def swapped(value):
    return lax.ppermute(value, "core", SWAP)


def move(value, axes, perm):
    if axes != Y:
        return lax.ppermute(value, axes, perm)
    outer, inner = lax.axis_size(Y[0]), lax.axis_size(Y[1])

    def flat(i):
        return i % inner * outer + i // inner

    return lax.ppermute(value, Y[::-1], [(flat(a), flat(b)) for a, b in perm])


def across(value):
    count = span(Y)
    return move(value, Y, [(i, count - 1 - i) for i in range(count)])


def repeated(value, axes):
    return jnp.broadcast_to(value[None], (span(axes),) + value.shape)


def copied(value, axes):
    return lax.all_to_all(repeated(value, axes), axes, 0, 0, tiled=True)


def summed(spread):
    return jnp.sum(spread, axis=0, dtype=F32)


def core_pair(mine, other):
    return (mine.astype(F32) + other.astype(F32)).astype(BF16)


def ring_pieces(keep, other, at, axes):
    count = span(axes)
    me = lax.axis_index(axes)

    def piece(step):
        index = lax.rem(me + step, count)
        mine = lax.dynamic_index_in_dim(keep, index, at, keepdims=False)
        theirs = lax.dynamic_index_in_dim(other, index, at, keepdims=False)
        return mine.astype(F32) + theirs.astype(F32)

    return [piece(step) if step == 0 else piece(step).astype(BF16) for step in range(count)]


def ring_sum(pieces, axes, rest, received):
    count = len(pieces)
    total = pieces[0]
    for step in range(1, count):
        perm = [(i, (i + step) % count) for i in range(count)]
        total = total + received(move(pieces[step], axes, perm)).astype(F32)
    total = total.astype(BF16)
    spread = total.reshape((span(rest),) + total.shape[-2:])
    return spread


def spread(value, axes):
    chunks = value.reshape((span(axes), -1, value.shape[-1]))
    return lax.all_to_all(chunks, axes, 0, 0, tiled=True)


def finish_all(place, pair, pair_other, attn, attn_other, grad, returned, down, up, qkv, out, total):
    total[...] = grad[...] + returned[...].astype(F32)
    blocks, tall, wide = attn.shape
    for half in range(2):
        keep = place[1] == half
        for block in range(blocks):
            value = jnp.where(keep, pair[block, 0, 0], pair_other[block, 0, 0]).astype(F32)
            down[block * tall : (block + 1) * tall, half * wide : (half + 1) * wide] = value
            value = jnp.where(keep, pair[block, 0, 1], pair_other[block, 0, 1]).astype(F32)
            start = (half * blocks + block) * wide
            up[:, start : start + wide] = value
            value = jnp.where(keep, attn[block], attn_other[block]).astype(F32)
            if start < qkv.shape[1]:
                qkv[:, start : start + wide] = value
            else:
                out[:, start - qkv.shape[1] : start - qkv.shape[1] + wide] = value


def finish_small(place, small, small_other, b_qv, b_up, *rest):
    wide = small.shape[1]
    flag = place[1] == 0
    first = jnp.where(flag, small[...], small_other[...])
    last = jnp.where(flag, small_other[...], small[...])
    rows = [first[k] for k in range(6)] + [last[k] for k in range(6)]
    for k in range(2):
        b_qv[k * wide : (k + 1) * wide] = rows[k]
    for k in range(4):
        b_up[k * wide : (k + 1) * wide] = rows[8 + k]
    for k, target in enumerate(rest):
        target[...] = rows[2 + k]


def on_device(
    tokens, w_qkv, b_qv, w_out, b_out, w_up, b_up, w_down, b_down,
    gain_one, shift_one, gain_two, shift_two, cotangent,
):
    rows, width = tokens.shape
    ff = w_up.shape[1]
    shard = lax.axis_index("y_hi")
    core = lax.axis_index("core")
    cell = lax.axis_index(PLANE)
    place = jnp.stack([shard, core]).astype(jnp.int32)
    plane, copies = span(PLANE), span(COPIES)

    half = w_qkv.shape[0] // 2
    nz, nx = lax.axis_size("z"), lax.axis_size("x")
    tall, wide = half // nx, ff // nz
    x, z = lax.axis_index("x"), lax.axis_index("z")
    first = core * half + x * tall
    up_cell = lax.dynamic_slice(w_up, (first, z * wide), (tall, wide))
    down_tall = ff // 4 // plane
    down_cell = lax.dynamic_slice_in_dim(
        w_down, core * (ff // 4) + cell * down_tall, down_tall, 0
    )
    cells = across(jnp.stack([up_cell, down_cell]))
    cells = repeated(cells, PLANE)
    attn_near = [lax.dynamic_slice_in_dim(w, core * half, half, 0) for w in (w_qkv, w_out)]
    x_prev = lax.ppermute(tokens, "y_hi", [(0, 1)])
    vectors = (b_qv, b_out, b_down, gain_one, shift_one, gain_two, shift_two, b_up)
    length = sum(vector.shape[0] for vector in vectors)
    packed, at = jnp.zeros((length,), F32), 0
    for vector in vectors:
        end = at + vector.shape[0]
        packed = packed + jnp.pad(vector.astype(F32), (at, length - end))
        at = end
    got = lax.ppermute(packed, "y_hi", SWAP)
    attn_near = across(after(jnp.concatenate(attn_near, axis=1), cells, x_prev, got))
    cells = lax.all_to_all(cells, PLANE, 0, 0, tiled=True)
    cells = cells.reshape((nz, nx) + cells.shape[1:])
    attn_far = swapped(attn_near)
    qkv = (w_qkv, attn_near, attn_far)
    out = (w_out, attn_near, attn_far)

    low = jnp.where(shard == 0, packed, got)
    high = jnp.where(shard == 0, got, packed)
    whole, at = [], 0
    for vector in vectors:
        size = vector.shape[0]
        whole.append(jnp.concatenate([low[at : at + size], high[at : at + size]])[None])
        at += size
    c_qv, c_out, c_down, g_one, s_one, g_two, s_two, c_up = whole
    dma = pltpu.SemaphoreType.DMA
    pairs = width // (2 * HEAD_DIM)

    normed, queries, keys, values, attended, log_total = call(
        forward_attention,
        [((2 * rows, width), BF16), ((rows, width), BF16), ((2 * rows, width), BF16),
         ((2 * rows, width), BF16), ((rows, width), BF16), ((pairs, 2 * rows), F32)],
        9 * 10**9, 8 * 10**6,
        [SM, VM, VM, ANY, ANY, ANY, VM, VM, VM],
        [pltpu.VMEM((width, 3 * width), BF16), dma((3,))],
    )(place, x_prev, tokens, *qkv, c_qv, g_one, s_one)

    cells = after(cells, attended)
    cells_far = swapped(cells)
    up = (w_up, cells, cells_far)
    down = (w_down, cells, cells_far)
    wide, tall = width // 2, width // 2 // (copies // 4)
    down_shape = (nx, span(Y), nz, tall, wide)
    middle, normed_two, hidden, activated, keep, send, grad_bd = call(
        forward_middle,
        [((rows, width), F32), ((rows, width), BF16), ((rows, ff), F32), ((rows, ff), BF16),
         (down_shape, BF16), (down_shape, BF16), ((1, width), F32)],
        12 * 10**9, 10**5,
        [SM, VM, VM, ANY, ANY, ANY, VM, VM, VM, ANY, ANY, ANY, VM, VM],
        [pltpu.VMEM((width, width), BF16), pltpu.VMEM((width, ff), BF16), dma((4 + 2 * plane,)),
         pltpu.VMEM((2,) + down_shape, BF16), dma((2,))],
        (4, 5),
    )(place, attended, tokens, *out, c_out, g_two, s_two, *up, c_up, cotangent)

    down_both = core_pair(keep, swapped(send)).reshape(-1, wide)
    down_part = lax.psum_scatter(down_both, "x", scatter_dimension=0, tiled=True)
    up_shape = (nz, 2, copies // 4, tall, wide)
    attn_shape = (2, copies // 4, nz, tall, wide)
    activated = after(activated, down_both)

    result, grad_hidden, keep, send, grad_bu = call(
        middle_back,
        [((rows, width), BF16), ((rows, ff), BF16), (up_shape, BF16), (up_shape, BF16),
         ((1, ff), F32)],
        13 * 10**9, 10**5,
        [SM, VM, VM, VM, VM, VM, ANY, ANY, ANY, VM],
        [pltpu.VMEM((ff, width), BF16), dma((1 + 2 * plane,)), pltpu.VMEM((2,) + up_shape, BF16), dma((2,))],
        (2, 3),
    )(place, cotangent, hidden, activated, normed_two, middle, *down, c_down)

    grid = (nz, span(Y), nx, tall, wide)
    up_pieces = ring_pieces(keep.reshape(grid), swapped(send).reshape(grid), 0, "z")
    grad_hidden = after(grad_hidden, *up_pieces[1:])

    grad_mid, grad_att, grad_wo, small = call(
        branch_back,
        [((rows, width), F32), ((rows, width), BF16), ((width, width), BF16), ((8, width), F32)],
        9 * 10**9, 10**5,
        [SM] + [VM] * 5 + [ANY] * 6,
        [pltpu.VMEM((width, ff), BF16), pltpu.VMEM((width, width), BF16), dma((4 + 2 * plane,))],
    )(place, cotangent, middle, grad_hidden, g_two, attended, *up, *out)

    down_part = after(down_part, grad_wo)
    down_sum = summed(spread(down_part, Y + ("z",))).astype(BF16)
    grad_att = after(grad_att, down_part)

    input_grad, prev_grad, keep, send, small, small_send = call(
        input_back,
        [((rows, width), F32), ((rows, width), BF16), (attn_shape, BF16), (attn_shape, BF16),
         ((2, 8, wide), F32), ((2, 8, wide), F32)],
        14 * 10**9, 10**5,
        [SM] + [VM] * 14 + [ANY] * 3,
        [pltpu.VMEM((2 * rows, 3 * width), BF16), pltpu.VMEM((width, 3 * width), BF16), dma((3,)),
         pltpu.VMEM((2,) + attn_shape, BF16), dma((2,))],
        (2, 3),
    )(place, x_prev, tokens, grad_mid, grad_att, grad_wo, normed, queries, keys, values,
      log_total, g_one, small, grad_bd, grad_bu, *qkv)

    chunks = (2 * copies, tall, wide)
    up_part = ring_sum(
        up_pieces, "z", Y + ("x",), lambda value: after(value, prev_grad, grad_mid)
    )
    attn_both = core_pair(keep, swapped(after(send, down_sum, up_part))).reshape(chunks)
    small = core_pair(small, swapped(small_send))
    small = jnp.broadcast_to(small[:, None], (2, copies) + small.shape[1:])
    attn_both = jnp.concatenate([attn_both, small.reshape((2 * copies,) + small.shape[2:])], axis=1)
    returned = lax.ppermute(prev_grad, "y_hi", [(1, 0)])
    up_part = after(up_part, down_sum, prev_grad)
    up_chunks = spread(up_part, Y + ("x",))
    up_chunks = after(up_chunks, attn_both, returned)
    up_sum = summed(up_chunks).astype(BF16)
    pair = jnp.stack([down_sum, up_sum])
    other = lax.ppermute(pair, "y_lo", SWAP)
    low_y = lax.axis_index("y_lo") == 0
    pair = jnp.stack([jnp.where(low_y, pair, other), jnp.where(low_y, other, pair)])
    attn_chunks = spread(after(attn_both, up_chunks), Y + ("x", "z"))
    attn_sum = summed(after(attn_chunks, pair))
    attn_sum, small = attn_sum[:tall].astype(BF16), attn_sum[tall:]
    other_small = swapped(small)
    sizes = [width, ff // 2] + [wide] * 6
    t_qv, t_up, t_out, t_down, t_g1, t_s1, t_g2, t_s2 = call(
        finish_small, [((size,), F32) for size in sizes], 10**5, 10**5, [SM, VM, VM]
    )(place, small, other_small)
    attn_mine = copied(after(attn_sum, t_qv), COPIES)
    attn_other = swapped(attn_mine)

    pair = lax.all_gather(pair.reshape(-1, wide), ("x", "z"), axis=0, tiled=True)
    pair = after(pair, attn_mine)
    pair = pair.reshape(plane, 2, 2, tall, wide)
    steps = copies // nz
    pair_block = pl.BlockSpec((nz, 1, 2, tall, wide), lambda i: (i % nx, i // nx, 0, 0, 0))
    attn_block = pl.BlockSpec((nz, tall, wide), lambda i: (i, 0, 0))
    shapes = ((ff // 2, width), (width // 2, ff), (width // 2, 3 * width), (width // 2, width))
    shapes += ((rows, width),)
    row_blocks = [
        pl.BlockSpec((high // steps, broad), lambda i: (i, 0)) for high, broad in shapes
    ]
    total_wd, total_wu, total_wqkv, total_wout, input_grad = pl.pallas_call(
        finish_all,
        grid=(steps,),
        out_shape=tuple(jax.ShapeDtypeStruct(shape, F32) for shape in shapes),
        in_specs=[SM, pair_block, pair_block, attn_block, attn_block] + [row_blocks[-1]] * 2,
        out_specs=tuple(row_blocks),
        compiler_params=pltpu.CompilerParams(vmem_limit_bytes=VMEM_LIMIT),
        cost_estimate=pl.CostEstimate(flops=14 * 10**9, bytes_accessed=10**5, transcendentals=0),
    )(place, pair, swapped(pair), attn_mine, attn_other, input_grad, returned)
    return (
        result,
        input_grad,
        total_wqkv,
        t_qv,
        total_wout,
        t_out,
        total_wu,
        t_up,
        total_wd,
        t_down,
        t_g1,
        t_s1,
        t_g2,
        t_s2,
    )


def solution(mesh):
    axes = ("x", "z", "y_lo", "core", "y_hi")
    fine = Mesh(mesh.devices.reshape(4, 4, 2, 2, 2), axes)
    split = P(axes, None)
    matrix, vector = P("y_hi", None), P("y_hi")
    params = (matrix, vector, matrix, vector, matrix, vector, matrix, vector) + (vector,) * 4
    return jax.shard_map(
        on_device,
        mesh=fine,
        in_specs=(split,) + params + (split,),
        out_specs=(split, split) + params,
        check_vma=False,
    )
```

```python
import functools
import jax
import jax.numpy as jnp
from jax import lax
from jax.experimental import pallas as pl
from jax.experimental.pallas import tpu as pltpu
from jax.sharding import Mesh
from jax.sharding import PartitionSpec as P

HEAD_DIM = 64
eps = 1e-05
F32 = jnp.float32
BF16 = jnp.bfloat16
VMEM_LIMIT = 63 * 1024 * 1024 + 512 * 1024


def dot_nn(left, right):
    return lax.dot_general(left, right, (((1,), (0,)), ((), ())), preferred_element_type=F32)


def dot_nt(left, right):
    return lax.dot_general(left, right, (((1,), (1,)), ((), ())), preferred_element_type=F32)


def dot_tn(left, right):
    return lax.dot_general(left, right, (((0,), (0,)), ((), ())), preferred_element_type=F32)


def normalise(values):
    center = jnp.mean(values, axis=-1, keepdims=True)
    centered = values - center
    spread = jnp.mean(centered * centered, axis=-1, keepdims=True)
    scale = lax.rsqrt(spread + eps)
    return centered * scale, scale


def norm_back(unit, scale, upstream, gain):
    q = upstream * gain
    return scale * (
        q
        - jnp.mean(q, axis=-1, keepdims=True)
        - unit * jnp.mean(q * unit, axis=-1, keepdims=True)
    )


def column_sum(values):
    return jnp.sum(values, axis=0, keepdims=True)


def two_heads(block):
    lane = lax.broadcasted_iota(jnp.int32, block.shape, 1)
    zero = jnp.zeros_like(block)
    return jnp.concatenate(
        [jnp.where(lane < HEAD_DIM, block, zero), jnp.where(lane < HEAD_DIM, zero, block)], axis=0
    )


def merge_heads(rows_t, count):
    row = lax.broadcasted_iota(jnp.int32, (2 * HEAD_DIM, count), 0)
    return jnp.transpose(
        jnp.where(row < HEAD_DIM, rows_t[:, :count], rows_t[:, count:]), (1, 0)
    )


def masked_scores(keys_two, queries_two, hidden_prev, count):
    scores = dot_nt(keys_two, queries_two)
    key = lax.broadcasted_iota(jnp.int32, (count, 2 * count), 0)
    query = lax.broadcasted_iota(jnp.int32, (count, 2 * count), 1)
    query = jnp.where(query >= count, query - count, query)
    prev = scores[:count] + hidden_prev
    here = jnp.where(key <= query, scores[count:], -1e30)
    return jnp.concatenate([prev, here], axis=0)


def assemble(place, parts, target, sems, first, weight=None, column=0):
    own = parts[0]
    half = own.shape[0]
    shard, core = place[0], place[1]
    quarter = half // 2
    away = (1 - shard) * half
    at = pl.multiple_of(shard * half, half)
    pieces = [(own, target.at[pl.ds(at, half)])]
    starts = (away + core * quarter, away + (1 - core) * quarter)
    for part, start in zip(parts[1:], starts):
        start = pl.multiple_of(start, quarter)
        if weight is None:
            part = part.at[:, column : column + target.shape[1]]
            pieces.append((part, target.at[pl.ds(start, quarter)]))
            continue
        outer, inner, _, tall, wide = part.shape
        for a in range(outer):
            for b in range(inner):
                row = b if weight == 0 else a * inner + b
                rows = pl.ds(pl.multiple_of(start + row * tall, tall), tall)
                left = a * wide if weight == 0 else 0
                pieces.append((part.at[a, b, weight], target.at[rows, left : left + wide]))
    copies = []
    for source, there in pieces:
        copies.append(pltpu.make_async_copy(source, there, sems.at[first + len(copies)]))
        copies[-1].start()
    return copies


def finish(copies):
    for copy in copies:
        copy.wait()


def store_rows(halves, chunk, value):
    _, across, _, along, tall, wide = halves.shape
    value = value.astype(BF16)
    for half in range(2):
        block = value[:, half * wide : (half + 1) * wide].reshape(across, along, tall, wide)
        halves[half, :, chunk] = block


def store_columns(halves, chunk, value, z_first):
    owners, rows, blocks = halves.shape[1:4]
    if z_first:
        blocks, owners, rows = owners, rows, blocks
    tall, wide = halves.shape[4:]
    value = value.astype(BF16)
    for part in range(value.shape[1] // wide):
        column = chunk * (value.shape[1] // wide) + part
        half, block = divmod(column, blocks)
        piece = value[:, part * wide : (part + 1) * wide].reshape(owners, rows, tall, wide)
        if z_first:
            halves[half, block] = piece
        else:
            halves[half, :, :, block] = piece


def hand_out(halves, core, keep, send, sems):
    copies = [
        pltpu.make_async_copy(halves.at[core], keep, sems.at[0]),
        pltpu.make_async_copy(halves.at[1 - core], send, sems.at[1]),
    ]
    for copy in copies:
        copy.start()
    return copies


def forward_attention(
    place, x_prev, x_here, own, near, far, b_qv, gain, shift,
    normed, queries, keys, values, attended, log_total, w_qkv, sems,
):
    copies = assemble(place, (own, near, far), w_qkv, sems, 0)
    rows, width = x_here.shape
    hidden_prev = jnp.where(place[0] > 0, 0.0, -1e30).astype(F32)
    for part, source in enumerate((x_prev, x_here)):
        unit, _ = normalise(source[...].astype(F32))
        normed[part * rows : (part + 1) * rows, :] = (unit * gain[...] + shift[...]).astype(BF16)
    finish(copies)
    here = normed[rows:, :]
    queries[...] = ((dot_nn(here, w_qkv[:, :width]) + b_qv[:, :width]) * 0.125).astype(BF16)
    keys[...] = dot_nn(normed[...], w_qkv[:, width : 2 * width]).astype(BF16)
    values[...] = (dot_nn(normed[...], w_qkv[:, 2 * width :]) + b_qv[:, width:]).astype(BF16)
    for pair in range(width // (2 * HEAD_DIM)):
        at = slice(pair * 2 * HEAD_DIM, (pair + 1) * 2 * HEAD_DIM)
        scores = masked_scores(keys[:, at], two_heads(queries[:, at]), hidden_prev, rows)
        top = jnp.max(scores, axis=0, keepdims=True)
        expo = jnp.exp(scores - top)
        total = jnp.sum(expo, axis=0, keepdims=True)
        probs_low = (expo * (1.0 / total)).astype(BF16)
        log_total[pair : pair + 1, :] = top + jnp.log(total)
        attended[:, at] = merge_heads(dot_tn(values[:, at], probs_low), rows).astype(BF16)


def forward_middle(
    place, attended, x_here, out_own, out_near, out_far, b_out, gain, shift,
    up_own, cells_near, cells_far, b_up, cotangent,
    middle, normed, hidden, activated, grad_w_keep, grad_w_send, grad_b_down, w_out, w_up, sems, halves, out_sems,
):
    out_copies = assemble(place, (out_own, out_near, out_far), w_out, sems, 0, column=3 * w_out.shape[0])
    up_copies = assemble(place, (up_own, cells_near, cells_far), w_up, sems, 3, 0)
    finish(out_copies)
    rows, width = x_here.shape
    mid = x_here[...].astype(F32) + (dot_nn(attended[...], w_out[...]) + b_out[...])
    middle[...] = mid
    unit, _ = normalise(mid)
    normed[...] = (unit * gain[...] + shift[...]).astype(BF16)
    finish(up_copies)
    for chunk in range(w_up.shape[1] // width):
        at = slice(chunk * width, (chunk + 1) * width)
        hid = dot_nn(normed[...], w_up[:, at]) + b_up[:, at]
        hidden[:, at] = hid
        low = jax.nn.gelu(hid, approximate=True).astype(BF16)
        activated[:, at] = low
        store_rows(halves, chunk, dot_tn(low, cotangent[...]))
    copies = hand_out(halves, place[1], grad_w_keep, grad_w_send, out_sems)
    grad_b_down[...] = column_sum(cotangent[...].astype(F32))
    finish(copies)


def gelu_slope(u):
    c = 0.7978845608028654
    t = jnp.tanh(c * (u + 0.044715 * (u * u * u)))
    return 0.5 * (1.0 + t) + 0.5 * u * (1.0 - t * t) * (c * (1.0 + 3.0 * 0.044715 * (u * u)))


def middle_back(
    place, cotangent, hidden, activated, normed, middle, own, near, far, b_down,
    result, grad_hidden, grad_w_keep, grad_w_send, grad_b_up, w_down, sems, halves, out_sems,
):
    finish(assemble(place, (own, near, far), w_down, sems, 0, 1))
    rows, width = middle.shape
    ct = cotangent[...]
    for chunk in range(w_down.shape[0] // width):
        at = slice(chunk * width, (chunk + 1) * width)
        grad_act = dot_nt(ct, w_down[at, :])
        grad_hid = (grad_act * gelu_slope(hidden[:, at])).astype(BF16)
        grad_hidden[:, at] = grad_hid
        grad_b_up[:, at] = column_sum(grad_hid.astype(F32))
        store_columns(halves, chunk, dot_tn(normed[...], grad_hid), True)
    copies = hand_out(halves, place[1], grad_w_keep, grad_w_send, out_sems)
    out = dot_nn(activated[...], w_down[...])
    result[...] = (middle[...] + (out + b_down[...])).astype(result.dtype)
    finish(copies)


def branch_back(
    place, cotangent, middle, grad_hidden, gain_two, attended,
    up_own, cells_near, cells_far, out_own, out_near, out_far,
    grad_mid, grad_att, grad_w_out, small,
    w_up, w_out, sems,
):
    up_copies = assemble(place, (up_own, cells_near, cells_far), w_up, sems, 3, 0)
    out_copies = assemble(place, (out_own, out_near, out_far), w_out, sems, 0, column=3 * w_out.shape[0])
    unit, scale = normalise(middle[...])
    finish(up_copies)
    grad_norm = dot_nt(grad_hidden[...], w_up[...])
    small[0:1, :] = column_sum(grad_norm * unit)
    small[1:2, :] = column_sum(grad_norm)
    grad = cotangent[...].astype(F32) + norm_back(unit, scale, grad_norm, gain_two[...])
    grad_mid[...] = grad
    grad_branch = grad.astype(BF16)
    small[2:3, :] = column_sum(grad_branch.astype(F32))
    small[3:8, :] = jnp.zeros((5, small.shape[1]), F32)
    finish(out_copies)
    grad_att[...] = dot_nt(grad_branch, w_out[...]).astype(BF16)
    grad_w_out[...] = dot_tn(attended[...], grad_branch).astype(BF16)


def input_back(
    place, x_prev, x_here, grad_mid, grad_att, grad_w_out, normed, queries, keys, values,
    log_total, gain_one, small, grad_b_down, grad_b_up, qkv_own, qkv_near, qkv_far,
    input_grad, prev_grad, grad_w_keep, grad_w_send, packed_keep, packed_send,
    grad_proj, w_qkv, sems, halves, out_sems,
):
    rows, width = x_here.shape
    qkv_copies = assemble(place, (qkv_own, qkv_near, qkv_far), w_qkv, sems, 0)
    hidden_prev = jnp.where(place[0] > 0, 0.0, -1e30).astype(F32)
    store_columns(halves, 3, grad_w_out[...], False)
    grad_proj[:rows, :width] = jnp.zeros((rows, width), BF16)
    for pair in range(width // (2 * HEAD_DIM)):
        at = slice(pair * 2 * HEAD_DIM, (pair + 1) * 2 * HEAD_DIM)
        queries_two = two_heads(queries[:, at])
        grads_two = two_heads(grad_att[:, at])
        scores = masked_scores(keys[:, at], queries_two, hidden_prev, rows)
        probs = jnp.exp(scores - log_total[pair : pair + 1, :])
        probs_low = probs.astype(BF16)
        grad_probs = dot_nt(values[:, at], grads_two)
        inner = jnp.sum(probs * grad_probs, axis=0, keepdims=True)
        grad_scores = (probs * (grad_probs - inner)).astype(BF16)
        first, last = pair * 2 * HEAD_DIM, (pair + 1) * 2 * HEAD_DIM
        grad_queries = merge_heads(dot_tn(keys[:, at], grad_scores), rows)
        grad_proj[rows:, at] = (grad_queries.astype(BF16) * 0.125).astype(BF16)
        grad_proj[:, width + first : width + last] = dot_nn(grad_scores, queries_two).astype(BF16)
        grad_proj[:, 2 * width + first : 2 * width + last] = dot_nn(probs_low, grads_two).astype(BF16)
    for chunk in range(3):
        at = slice(chunk * width, (chunk + 1) * width)
        store_columns(halves, chunk, dot_tn(normed[...], grad_proj[:, at]), False)
    copies = hand_out(halves, place[1], grad_w_keep, grad_w_send, out_sems)
    b_query = column_sum(grad_proj[:, :width].astype(F32))
    b_value = column_sum(grad_proj[:, 2 * width :].astype(F32))
    gain_sum = jnp.zeros((1, width), F32)
    shift_sum = jnp.zeros((1, width), F32)
    finish(qkv_copies)
    for part, source in enumerate((x_prev, x_here)):
        at = slice(part * rows, (part + 1) * rows)
        first = (1 - part) * width
        grad_norm = dot_nt(grad_proj[at, first:], w_qkv[:, first:])
        unit, scale = normalise(source[...].astype(F32))
        gain_sum = gain_sum + column_sum(grad_norm * unit)
        shift_sum = shift_sum + column_sum(grad_norm)
        grad_in = norm_back(unit, scale, grad_norm, gain_one[...])
        if part == 0:
            prev_grad[...] = grad_in.astype(prev_grad.dtype)
        else:
            input_grad[...] = grad_mid[...] + grad_in
    part = width // 2
    shared = (small[2:3, :], grad_b_down[...], gain_sum, shift_sum, small[0:1, :], small[1:2, :])
    for owner, bias in enumerate((b_query, b_value)):
        at = slice(owner * part, (owner + 1) * part)
        rows_of = [bias[:, :part], bias[:, part:]]
        rows_of += [vector[:, at] for vector in shared]
        first = owner * 4 * part
        rows_of += [grad_b_up[:, first + k * part : first + (k + 1) * part] for k in range(4)]
        zeros = jnp.zeros((2, part), F32)
        blocks = [
            jnp.concatenate(rows_of[6 * half : 6 * half + 6] + [zeros], axis=0)
            for half in range(2)
        ]
        mine = place[1] == 0
        packed_keep[owner] = jnp.where(mine, blocks[0], blocks[1])
        packed_send[owner] = jnp.where(mine, blocks[1], blocks[0])
    finish(copies)


VM = pl.BlockSpec(memory_space=pltpu.VMEM)
SM = pl.BlockSpec(memory_space=pltpu.SMEM)
ANY = pl.BlockSpec(memory_space=pl.ANY)


def call(body, outs, flops, moved, in_specs, scratch=(), away=()):
    return pl.pallas_call(
        body,
        out_shape=tuple(jax.ShapeDtypeStruct(s, d) for s, d in outs),
        in_specs=in_specs,
        out_specs=tuple(ANY if k in away else VM for k in range(len(outs))),
        scratch_shapes=list(scratch),
        compiler_params=pltpu.CompilerParams(vmem_limit_bytes=VMEM_LIMIT),
        cost_estimate=pl.CostEstimate(flops=flops, bytes_accessed=moved, transcendentals=0),
    )


Y = ("y_hi", "y_lo")
COPIES = ("y_lo", "x", "z")
PLANE = ("z", "x")
SWAP = [(0, 1), (1, 0)]


def span(axes):
    count = 1
    for axis in axes:
        count *= lax.axis_size(axis)
    return count


def after(value, *tokens):
    def body(*refs):
        pass

    return pl.pallas_call(
        body,
        out_shape=jax.ShapeDtypeStruct(value.shape, value.dtype),
        in_specs=[ANY] * (1 + len(tokens)),
        out_specs=ANY,
        input_output_aliases={0: 0},
        compiler_params=pltpu.CompilerParams(vmem_limit_bytes=VMEM_LIMIT),
    )(value, *tokens)


def swapped(value):
    return lax.ppermute(value, "core", SWAP)


def move(value, axes, perm):
    if axes != Y:
        return lax.ppermute(value, axes, perm)
    outer, inner = lax.axis_size(Y[0]), lax.axis_size(Y[1])

    def flat(i):
        return i % inner * outer + i // inner

    return lax.ppermute(value, Y[::-1], [(flat(a), flat(b)) for a, b in perm])


def across(value):
    count = span(Y)
    return move(value, Y, [(i, count - 1 - i) for i in range(count)])


def repeated(value, axes):
    return jnp.broadcast_to(value[None], (span(axes),) + value.shape)


def copied(value, axes):
    return lax.all_to_all(repeated(value, axes), axes, 0, 0, tiled=True)


def summed(spread):
    return jnp.sum(spread, axis=0, dtype=F32)


def core_pair(mine, other):
    return (mine.astype(F32) + other.astype(F32)).astype(BF16)


def ring_pieces(keep, other, at, axes):
    count = span(axes)
    me = lax.axis_index(axes)

    def piece(step):
        index = lax.rem(me + step, count)
        mine = lax.dynamic_index_in_dim(keep, index, at, keepdims=False)
        theirs = lax.dynamic_index_in_dim(other, index, at, keepdims=False)
        return mine.astype(F32) + theirs.astype(F32)

    return [piece(step) if step == 0 else piece(step).astype(BF16) for step in range(count)]


def ring_sum(pieces, axes, rest, received):
    count = len(pieces)
    total = pieces[0]
    for step in range(1, count):
        perm = [(i, (i + step) % count) for i in range(count)]
        total = total + received(move(pieces[step], axes, perm)).astype(F32)
    total = total.astype(BF16)
    spread = total.reshape((span(rest),) + total.shape[-2:])
    return spread


def spread(value, axes):
    chunks = value.reshape((span(axes), -1, value.shape[-1]))
    return lax.all_to_all(chunks, axes, 0, 0, tiled=True)


def finish_all(place, pair, pair_other, attn, attn_other, grad, returned, down, up, qkv, out, total):
    total[...] = grad[...] + returned[...].astype(F32)
    blocks, tall, wide = attn.shape
    for half in range(2):
        keep = place[1] == half
        for block in range(blocks):
            value = jnp.where(keep, pair[block, 0, 0], pair_other[block, 0, 0]).astype(F32)
            down[block * tall : (block + 1) * tall, half * wide : (half + 1) * wide] = value
            value = jnp.where(keep, pair[block, 0, 1], pair_other[block, 0, 1]).astype(F32)
            start = (half * blocks + block) * wide
            up[:, start : start + wide] = value
            value = jnp.where(keep, attn[block], attn_other[block]).astype(F32)
            if start < qkv.shape[1]:
                qkv[:, start : start + wide] = value
            else:
                out[:, start - qkv.shape[1] : start - qkv.shape[1] + wide] = value


def finish_small(place, small, small_other, b_qv, b_up, *rest):
    wide = small.shape[1]
    flag = place[1] == 0
    first = jnp.where(flag, small[...], small_other[...])
    last = jnp.where(flag, small_other[...], small[...])
    rows = [first[k] for k in range(6)] + [last[k] for k in range(6)]
    for k in range(2):
        b_qv[k * wide : (k + 1) * wide] = rows[k]
    for k in range(4):
        b_up[k * wide : (k + 1) * wide] = rows[8 + k]
    for k, target in enumerate(rest):
        target[...] = rows[2 + k]


def on_device(
    tokens, w_qkv, b_qv, w_out, b_out, w_up, b_up, w_down, b_down,
    gain_one, shift_one, gain_two, shift_two, cotangent,
):
    rows, width = tokens.shape
    ff = w_up.shape[1]
    shard = lax.axis_index("y_hi")
    core = lax.axis_index("core")
    cell = lax.axis_index(PLANE)
    place = jnp.stack([shard, core]).astype(jnp.int32)
    plane, copies = span(PLANE), span(COPIES)

    half = w_qkv.shape[0] // 2
    nz, nx = lax.axis_size("z"), lax.axis_size("x")
    tall, wide = half // nx, ff // nz
    x, z = lax.axis_index("x"), lax.axis_index("z")
    first = core * half + x * tall
    up_cell = lax.dynamic_slice(w_up, (first, z * wide), (tall, wide))
    down_tall = ff // 4 // plane
    down_cell = lax.dynamic_slice_in_dim(
        w_down, core * (ff // 4) + cell * down_tall, down_tall, 0
    )
    cells = across(jnp.stack([up_cell, down_cell]))
    cells = repeated(cells, PLANE)
    attn_near = [lax.dynamic_slice_in_dim(w, core * half, half, 0) for w in (w_qkv, w_out)]
    x_prev = lax.ppermute(tokens, "y_hi", [(0, 1)])
    vectors = (b_qv, b_out, b_down, gain_one, shift_one, gain_two, shift_two, b_up)
    length = sum(vector.shape[0] for vector in vectors)
    packed, at = jnp.zeros((length,), F32), 0
    for vector in vectors:
        end = at + vector.shape[0]
        packed = packed + jnp.pad(vector.astype(F32), (at, length - end))
        at = end
    got = lax.ppermute(packed, "y_hi", SWAP)
    attn_near = across(after(jnp.concatenate(attn_near, axis=1), cells, x_prev, got))
    cells = lax.all_to_all(cells, PLANE, 0, 0, tiled=True)
    cells = cells.reshape((nz, nx) + cells.shape[1:])
    attn_far = swapped(attn_near)
    qkv = (w_qkv, attn_near, attn_far)
    out = (w_out, attn_near, attn_far)

    low = jnp.where(shard == 0, packed, got)
    high = jnp.where(shard == 0, got, packed)
    whole, at = [], 0
    for vector in vectors:
        size = vector.shape[0]
        whole.append(jnp.concatenate([low[at : at + size], high[at : at + size]])[None])
        at += size
    c_qv, c_out, c_down, g_one, s_one, g_two, s_two, c_up = whole
    dma = pltpu.SemaphoreType.DMA
    pairs = width // (2 * HEAD_DIM)

    normed, queries, keys, values, attended, log_total = call(
        forward_attention,
        [((2 * rows, width), BF16), ((rows, width), BF16), ((2 * rows, width), BF16),
         ((2 * rows, width), BF16), ((rows, width), BF16), ((pairs, 2 * rows), F32)],
        9 * 10**9, 8 * 10**6,
        [SM, VM, VM, ANY, ANY, ANY, VM, VM, VM],
        [pltpu.VMEM((width, 3 * width), BF16), dma((3,))],
    )(place, x_prev, tokens, *qkv, c_qv, g_one, s_one)

    cells = after(cells, attended)
    cells_far = swapped(cells)
    up = (w_up, cells, cells_far)
    down = (w_down, cells, cells_far)
    wide, tall = width // 2, width // 2 // (copies // 4)
    down_shape = (nx, span(Y), nz, tall, wide)
    middle, normed_two, hidden, activated, keep, send, grad_bd = call(
        forward_middle,
        [((rows, width), F32), ((rows, width), BF16), ((rows, ff), F32), ((rows, ff), BF16),
         (down_shape, BF16), (down_shape, BF16), ((1, width), F32)],
        12 * 10**9, 10**5,
        [SM, VM, VM, ANY, ANY, ANY, VM, VM, VM, ANY, ANY, ANY, VM, VM],
        [pltpu.VMEM((width, width), BF16), pltpu.VMEM((width, ff), BF16), dma((4 + 2 * plane,)),
         pltpu.VMEM((2,) + down_shape, BF16), dma((2,))],
        (4, 5),
    )(place, attended, tokens, *out, c_out, g_two, s_two, *up, c_up, cotangent)

    down_both = core_pair(keep, swapped(send)).reshape(-1, wide)
    down_part = lax.psum_scatter(down_both, "x", scatter_dimension=0, tiled=True)
    up_shape = (nz, 2, copies // 4, tall, wide)
    attn_shape = (2, copies // 4, nz, tall, wide)
    activated = after(activated, down_both)

    result, grad_hidden, keep, send, grad_bu = call(
        middle_back,
        [((rows, width), BF16), ((rows, ff), BF16), (up_shape, BF16), (up_shape, BF16),
         ((1, ff), F32)],
        13 * 10**9, 10**5,
        [SM, VM, VM, VM, VM, VM, ANY, ANY, ANY, VM],
        [pltpu.VMEM((ff, width), BF16), dma((1 + 2 * plane,)), pltpu.VMEM((2,) + up_shape, BF16), dma((2,))],
        (2, 3),
    )(place, cotangent, hidden, activated, normed_two, middle, *down, c_down)

    grid = (nz, span(Y), nx, tall, wide)
    up_pieces = ring_pieces(keep.reshape(grid), swapped(send).reshape(grid), 0, "z")
    grad_hidden = after(grad_hidden, *up_pieces[1:])

    grad_mid, grad_att, grad_wo, small = call(
        branch_back,
        [((rows, width), F32), ((rows, width), BF16), ((width, width), BF16), ((8, width), F32)],
        9 * 10**9, 10**5,
        [SM] + [VM] * 5 + [ANY] * 6,
        [pltpu.VMEM((width, ff), BF16), pltpu.VMEM((width, width), BF16), dma((4 + 2 * plane,))],
    )(place, cotangent, middle, grad_hidden, g_two, attended, *up, *out)

    down_part = after(down_part, grad_wo)
    down_sum = summed(spread(down_part, Y + ("z",))).astype(BF16)
    grad_att = after(grad_att, down_part)

    input_grad, prev_grad, keep, send, small, small_send = call(
        input_back,
        [((rows, width), F32), ((rows, width), BF16), (attn_shape, BF16), (attn_shape, BF16),
         ((2, 8, wide), F32), ((2, 8, wide), F32)],
        14 * 10**9, 10**5,
        [SM] + [VM] * 14 + [ANY] * 3,
        [pltpu.VMEM((2 * rows, 3 * width), BF16), pltpu.VMEM((width, 3 * width), BF16), dma((3,)),
         pltpu.VMEM((2,) + attn_shape, BF16), dma((2,))],
        (2, 3),
    )(place, x_prev, tokens, grad_mid, grad_att, grad_wo, normed, queries, keys, values,
      log_total, g_one, small, grad_bd, grad_bu, *qkv)

    chunks = (2 * copies, tall, wide)
    up_part = ring_sum(
        up_pieces, "z", Y + ("x",), lambda value: after(value, prev_grad, grad_mid)
    )
    attn_both = core_pair(keep, swapped(after(send, down_sum, up_part))).reshape(chunks)
    small = core_pair(small, swapped(small_send))
    small = jnp.broadcast_to(small[:, None], (2, copies) + small.shape[1:])
    attn_both = jnp.concatenate([attn_both, small.reshape((2 * copies,) + small.shape[2:])], axis=1)
    returned = lax.ppermute(prev_grad, "y_hi", [(1, 0)])
    up_part = after(up_part, down_sum, prev_grad)
    up_chunks = spread(up_part, Y + ("x",))
    up_chunks = after(up_chunks, attn_both, returned)
    up_sum = summed(up_chunks).astype(BF16)
    pair = jnp.stack([down_sum, up_sum])
    other = lax.ppermute(pair, "y_lo", SWAP)
    low_y = lax.axis_index("y_lo") == 0
    pair = jnp.stack([jnp.where(low_y, pair, other), jnp.where(low_y, other, pair)])
    attn_chunks = spread(after(attn_both, up_chunks), Y + ("x", "z"))
    attn_sum = summed(after(attn_chunks, pair))
    attn_sum, small = attn_sum[:tall].astype(BF16), attn_sum[tall:]
    other_small = swapped(small)
    sizes = [width, ff // 2] + [wide] * 6
    t_qv, t_up, t_out, t_down, t_g1, t_s1, t_g2, t_s2 = call(
        finish_small, [((size,), F32) for size in sizes], 10**5, 10**5, [SM, VM, VM]
    )(place, small, other_small)
    attn_mine = copied(attn_sum, COPIES)
    attn_other = swapped(attn_mine)

    pair = lax.all_gather(pair.reshape(-1, wide), ("x", "z"), axis=0, tiled=True)
    pair = after(pair, attn_mine)
    pair = pair.reshape(plane, 2, 2, tall, wide)
    steps = copies // nz
    pair_block = pl.BlockSpec((nz, 1, 2, tall, wide), lambda i: (i % nx, i // nx, 0, 0, 0))
    attn_block = pl.BlockSpec((nz, tall, wide), lambda i: (i, 0, 0))
    shapes = ((ff // 2, width), (width // 2, ff), (width // 2, 3 * width), (width // 2, width))
    shapes += ((rows, width),)
    row_blocks = [
        pl.BlockSpec((high // steps, broad), lambda i: (i, 0)) for high, broad in shapes
    ]
    total_wd, total_wu, total_wqkv, total_wout, input_grad = pl.pallas_call(
        finish_all,
        grid=(steps,),
        out_shape=tuple(jax.ShapeDtypeStruct(shape, F32) for shape in shapes),
        in_specs=[SM, pair_block, pair_block, attn_block, attn_block] + [row_blocks[-1]] * 2,
        out_specs=tuple(row_blocks),
        compiler_params=pltpu.CompilerParams(vmem_limit_bytes=VMEM_LIMIT),
        cost_estimate=pl.CostEstimate(flops=14 * 10**9, bytes_accessed=10**5, transcendentals=0),
    )(place, pair, swapped(pair), attn_mine, attn_other, input_grad, returned)
    return (
        result,
        input_grad,
        total_wqkv,
        t_qv,
        total_wout,
        t_out,
        total_wu,
        t_up,
        total_wd,
        t_down,
        t_g1,
        t_s1,
        t_g2,
        t_s2,
    )


def solution(mesh):
    axes = ("x", "z", "y_lo", "core", "y_hi")
    fine = Mesh(mesh.devices.reshape(4, 4, 2, 2, 2), axes)
    split = P(axes, None)
    matrix, vector = P("y_hi", None), P("y_hi")
    params = (matrix, vector, matrix, vector, matrix, vector, matrix, vector) + (vector,) * 4
    return jax.shard_map(
        on_device,
        mesh=fine,
        in_specs=(split,) + params + (split,),
        out_specs=(split, split) + params,
        check_vma=False,
    )
```
